32 devices in a mesh: row: 4 (over y, core), col: 8 (over z, x).
Axes of the slice: x: 2, y: 2, z: 4, core: 2. Of those that a mesh axis runs over, the one named last changes fastest.
Arguments:
- vectors: bfloat16 [32, 8192], P(None, ('col', 'row')), may hold values from -6 to 6
- tile_data: bfloat16 [2048, 128, 128], P(('col', 'row')), may hold values from -0.09375 to 0.09375
- tile_row: int32 [2048], P(('col', 'row')), may hold values from 0 to 7
- tile_offset: int32 [2048], P(('col', 'row')), may hold values from 0 to 7
- tile_live: int32 [32], P(('col', 'row')), may hold values from 1 to 64, as said below
- damp_center: float32 [1], replicated, may hold values from -0.5 to 0.5
- damp_radius: float32 [1], replicated, may hold values from 1 to 2
Outputs:
- first_degree: bfloat16 [32, 8192], P(None, ('col', 'row'))
- second_degree: float32 [32, 8192], P(None, ('col', 'row'))
The draws below stay inside these ranges and needn't reach their ends.
Inputs may be any that keep to these rules, and one draw needn't show every extreme that they name: `tile_live`: every device has at least one live slot, and some device has all 64.
All inputs are finite; a program needn't handle non-finite values.
Results may differ from the reference program's by a relative error of at most 0.0024.
Values may be sent and summed in bfloat16 or wider, within the bound.
No kernel may reach another device: no remote copies, remote signals or barrier semaphores. Data moves between devices by JAX's collectives and lax.ppermute only.
A program may use at most 64 MiB of HBM per device.

```python
import jax
import jax.numpy as jnp
from jax import lax

BS = 128
NV = 32
BLK_DEV = 2
TILES_DEV = 64
RANGE = 8
NB = 64
TILES = 2048
N_ROW = 4
N_COL = 8


def draw_tile_live(key, part):
    key = jax.random.fold_in(key, 7)
    key_expo, key_jitter, key_full = jax.random.split(key, 3)
    count_all = N_COL * N_ROW
    exponent = jax.random.randint(key_expo, (count_all,), 0, 4)
    base_count = TILES_DEV // jnp.power(2, exponent).astype(jnp.int32)
    jitter = jax.random.randint(key_jitter, (count_all,), 0, max(TILES_DEV // 16, 1) + 1)
    counts = jnp.maximum(base_count - jitter, 1)
    full_slot = jax.random.randint(key_full, (), 0, count_all)
    counts = counts.at[full_slot].set(TILES_DEV)
    return counts.astype(jnp.int32)


def set_ends(array, stream_key, least, top_value):
    dims = array.shape
    place = [jax.random.randint(jax.random.fold_in(stream_key, axis), (), 0, dims[axis]) for axis in range(len(dims))]
    array = array.at[tuple(place)].set(least)
    longest = dims.index(max(dims))
    place[longest] = (place[longest] + 1) % dims[longest]
    return array.at[tuple(place)].set(top_value)


def shard_levels(own_key, shape, shards, least, top_value):
    def one(dim, blocks):
        draws = jax.random.uniform(jax.random.fold_in(jax.random.fold_in(own_key, 6), dim), (blocks,), jnp.float32, least / len(shards), top_value / len(shards))
        return jnp.repeat(jnp.exp(draws), shape[dim] // blocks).reshape((-1,) + (1,) * (len(shape) - dim - 1))

    gain = one(*shards[0])
    for cut in shards[1:]:
        gain = gain * one(*cut)
    return gain


def scatter_about(own_key, dims, width, most, cuts=(), kind=jnp.bfloat16):
    result = jax.random.normal(own_key, dims, jnp.float32) * width
    if len(cuts) > 0:
        result = shard_levels(own_key, dims, cuts, -0.22, 0.18) * result
    return jnp.clip(result, min=-most, max=most).astype(kind)


def setup_inputs(seed: int = 0) -> dict:
    keys = jax.random.split(jax.random.key(seed), 8)
    vectors = scatter_about(keys[0], (NV, NB * BS), 1.0, 6.0, ((1, 32),))
    tile_data = scatter_about(keys[1], (TILES, BS, BS), (BS * TILES_DEV // BLK_DEV) ** -0.5, 0.09375, ((0, 32),))
    tile_row = set_ends(jax.random.randint(keys[2], (TILES,), 0, RANGE), jax.random.fold_in(keys[2], 1), 0, RANGE - 1).astype(jnp.int32)
    tile_offset = set_ends(jax.random.randint(keys[3], (TILES,), 0, RANGE), jax.random.fold_in(keys[3], 1), 0, RANGE - 1).astype(jnp.int32)
    tile_live = draw_tile_live(jax.random.fold_in(keys[7], 71), 0)
    damp_center = jnp.clip(jax.random.uniform(keys[5], (1,), jnp.float32, -0.5, 0.5), -0.5, 0.5)
    damp_radius = jnp.clip(jax.random.uniform(keys[6], (1,), jnp.float32, 1.0, 2.0), 1.0, 2.0)
    return {"vectors": vectors, "tile_data": tile_data, "tile_row": tile_row, "tile_offset": tile_offset, "tile_live": tile_live, "damp_center": damp_center, "damp_radius": damp_radius}


def apply_operator(vectors_bf, tile_data, tile_row, tile_offset, tile_live):
    vec_count = vectors_bf.shape[0]
    range_blocks = BLK_DEV * N_ROW
    total_cells = BLK_DEV * N_ROW * N_COL * BS
    padded = jnp.concatenate([vectors_bf.astype(jnp.float32), jnp.zeros((vec_count, range_blocks * BS), jnp.float32)], axis=1)
    slot_ids = jnp.arange(2 * range_blocks, dtype=jnp.int32)
    slot_index = jnp.arange(TILES_DEV, dtype=jnp.int32)

    def add_device(totals, device):
        group = device // N_ROW
        first_cell = (group * range_blocks * BS).astype(jnp.int32)
        window = lax.dynamic_slice_in_dim(padded, first_cell, 2 * range_blocks * BS, 1)
        blocks = window.reshape(vec_count, 2 * range_blocks, BS)
        first_slot = (device * TILES_DEV).astype(jnp.int32)
        tiles_here = lax.dynamic_slice_in_dim(tile_data, first_slot, TILES_DEV, 0).astype(jnp.float32)
        tile_rows = lax.dynamic_slice_in_dim(tile_row, first_slot, TILES_DEV, 0)
        tile_cols = tile_rows + lax.dynamic_slice_in_dim(tile_offset, first_slot, TILES_DEV, 0)
        live_mask = (slot_index < tile_live[device]).astype(jnp.float32)
        picked_col = jnp.take(blocks, tile_cols, axis=1)
        picked_row = jnp.take(blocks, tile_rows, axis=1)
        direct = jnp.einsum('vkb,kab->vka', picked_col, tiles_here, precision=lax.Precision.HIGHEST)
        mirrored = jnp.einsum('vka,kab->vkb', picked_row, tiles_here, precision=lax.Precision.HIGHEST)
        to_row = (tile_rows[:, None] == slot_ids[None, :]).astype(jnp.float32) * live_mask[:, None]
        to_col = (tile_cols[:, None] == slot_ids[None, :]).astype(jnp.float32) * live_mask[:, None]
        partial_value = jnp.einsum('kr,vkb->vrb', to_row, direct, precision=lax.Precision.HIGHEST)
        partial_value = partial_value + jnp.einsum('kr,vkb->vrb', to_col, mirrored, precision=lax.Precision.HIGHEST)
        partial_value = partial_value.reshape(vec_count, 2 * range_blocks * BS)
        current = lax.dynamic_slice_in_dim(totals, first_cell, 2 * range_blocks * BS, 1)
        totals = lax.dynamic_update_slice_in_dim(totals, current + partial_value, first_cell, 1)
        return totals, None

    totals = jnp.zeros((vec_count, total_cells + range_blocks * BS), jnp.float32)
    totals, _ = lax.scan(add_device, totals, jnp.arange(N_ROW * N_COL, dtype=jnp.int32))
    return totals[:, :total_cells]


def reference(vectors, tile_data, tile_row, tile_offset, tile_live, damp_center, damp_radius):
    center = damp_center[0]
    radius = damp_radius[0]
    vectors_f = vectors.astype(jnp.float32)
    image = apply_operator(vectors, tile_data, tile_row, tile_offset, tile_live)
    first_degree = ((image - center * vectors_f) / radius).astype(jnp.bfloat16)
    second_image = apply_operator(first_degree, tile_data, tile_row, tile_offset, tile_live)
    second_degree = 2.0 * (second_image - center * first_degree.astype(jnp.float32)) / radius - vectors_f
    return first_degree, second_degree
```

```python
import functools

import jax
import jax.numpy as jnp
from jax import lax
from jax.experimental import pallas as pl
from jax.experimental.pallas import tpu as pltpu
from jax.sharding import PartitionSpec as P

VMEM = pl.BlockSpec(memory_space=pltpu.VMEM)
SMEM = pl.BlockSpec(memory_space=pltpu.SMEM)
AXES = ("row", "col")


def row_swap(block, distance):
    rows, cols = lax.axis_size("row"), lax.axis_size("col")
    route = [(r * cols + c, (r ^ distance) * cols + c) for r in range(rows) for c in range(cols)]
    return lax.ppermute(block, AXES, route)


def pair_swap(block, odd):
    rows, cols = lax.axis_size("row"), lax.axis_size("col")
    route = []
    for r in range(rows):
        for c in range(odd, cols - 1, 2):
            route.append((r * cols + c, (r ^ 1) * cols + c + 1))
            route.append((r * cols + c + 1, (r ^ 1) * cols + c))
    return lax.ppermute(block, AXES, route)


def select_kernel(own_ref, even_ref, odd_ref, out_ref):
    parity = lax.rem(lax.axis_index("col"), 2)
    out_ref[0] = own_ref[...]

    @pl.when(parity == 0)
    def _():
        out_ref[1] = even_ref[...]

    @pl.when(parity == 1)
    def _():
        out_ref[1] = odd_ref[...]


def tiles_kernel(rows, blk, tile_row_ref, tile_offset_ref, live_ref, tile_ref, *refs):
    parts = refs[:rows]
    outs = refs[rows : 2 * rows]
    window, total = refs[2 * rows :]
    span = rows * blk
    size = tile_ref.shape[-1]
    me = lax.axis_index("row")
    for s in range(rows):
        for half in range(2):
            for b in range(blk):
                window[half * span + s * blk + b] = parts[s][half, :, b * size : (b + 1) * size]
    total[...] = jnp.zeros_like(total)
    own_mask = me * blk
    next_mask = (me ^ 1) * blk
    live = live_ref[0]

    def tile(k):
        i = tile_row_ref[k]
        j = i + tile_offset_ref[k]
        at_i = i ^ own_mask
        at_j = jnp.where(j < span, j ^ own_mask, span + ((j - span) ^ next_mask))
        to_i = jnp.where(k < live, at_i, 2 * span)
        to_j = jnp.where(k < live, at_j, 2 * span)
        u = tile_ref[k]
        direct = lax.dot_general(
            window[at_j], u, (((1,), (1,)), ((), ())), preferred_element_type=jnp.float32
        )
        mirrored = jnp.dot(window[at_i], u, preferred_element_type=jnp.float32)
        return to_i, to_j, direct, mirrored

    group = 8

    def body(g, carry):
        done = [tile(g * group + k) for k in range(group)]
        for to_i, to_j, direct, mirrored in done:
            total[to_i] += direct
            total[to_j] += mirrored
        return carry

    lax.fori_loop(0, tile_ref.shape[0] // group, body, 0)
    for s in range(rows):
        for half in range(2):
            for b in range(blk):
                outs[s][half, :, b * size : (b + 1) * size] = total[half * span + s * blk + b]


def add_kernel(rows, *refs):
    parts, (even_ref, odd_ref, sum_ref) = refs[:rows], refs[rows:]
    total = parts[0][...]
    for s in range(1, rows):
        total = total + parts[s][...]
    sum_ref[...] = total
    parity = lax.rem(lax.axis_index("col"), 2)

    @pl.when(parity == 0)
    def _():
        even_ref[...] = total[1]
        odd_ref[...] = total[0]

    @pl.when(parity == 1)
    def _():
        even_ref[...] = total[0]
        odd_ref[...] = total[1]


def first_kernel(center_ref, radius_ref, vectors_ref, sum_ref, even_ref, odd_ref, out_ref, first_ref):
    col = lax.axis_index("col")
    parity = lax.rem(col, 2)
    center, radius = center_ref[0], radius_ref[0]

    def degree(image, vectors):
        return ((image - center * vectors.astype(jnp.float32)) / radius).astype(jnp.bfloat16)

    def both(from_previous, from_next):
        own = degree(sum_ref[0] + from_previous[...], vectors_ref[0])
        out_ref[0] = own
        first_ref[...] = own
        inside = col < lax.axis_size("col") - 1
        beyond = degree(sum_ref[1] + from_next[...], vectors_ref[1])
        out_ref[1] = jnp.where(inside, beyond, jnp.zeros_like(beyond))

    @pl.when(parity == 0)
    def _():
        both(odd_ref, even_ref)

    @pl.when(parity == 1)
    def _():
        both(even_ref, odd_ref)


def second_kernel(center_ref, radius_ref, vectors_ref, first_ref, sum_ref, even_ref, odd_ref, out_ref):
    parity = lax.rem(lax.axis_index("col"), 2)
    center, radius = center_ref[0], radius_ref[0]

    def finish(from_previous):
        image = sum_ref[...] + from_previous[...]
        first = first_ref[...].astype(jnp.float32)
        out_ref[...] = 2.0 * (image - center * first) / radius - vectors_ref[...].astype(jnp.float32)

    @pl.when(parity == 0)
    def _():
        finish(odd_ref)

    @pl.when(parity == 1)
    def _():
        finish(even_ref)


def add_last_kernel(rows, *refs):
    parts, (low_ref, up_ref) = refs[:rows], refs[rows:]
    total = parts[0][...]
    for s in range(1, rows):
        total = total + parts[s][...]
    low_ref[...] = total[0]
    up_ref[...] = total[1]


def local(vectors, tile_data, tile_row, tile_offset, tile_live, damp_center, damp_radius):
    rows = lax.axis_size("row")
    count, width = vectors.shape
    size = tile_data.shape[-1]
    blk = width // size
    f32, bf16 = jnp.float32, jnp.bfloat16
    piece = jax.ShapeDtypeStruct((2, count, width), f32)
    single = jax.ShapeDtypeStruct((count, width), f32)
    pair_bf = jax.ShapeDtypeStruct((2, count, width), bf16)

    def apply(pair):
        gathered = [pair] + [row_swap(pair, s) for s in range(1, rows)]
        parts = pl.pallas_call(
            functools.partial(tiles_kernel, rows, blk),
            out_shape=[piece] * rows,
            in_specs=[SMEM] * 3 + [VMEM] * (1 + rows),
            out_specs=[VMEM] * rows,
            scratch_shapes=[
                pltpu.VMEM((2 * rows * blk, count, size), bf16),
                pltpu.VMEM((2 * rows * blk + 1, count, size), f32),
            ],
            name="tiles",
        )(tile_row, tile_offset, tile_live, tile_data, *gathered)
        return [parts[0]] + [row_swap(parts[s], s) for s in range(1, rows)]

    pair = pl.pallas_call(
        select_kernel, out_shape=pair_bf, in_specs=[VMEM] * 3, out_specs=VMEM, name="select"
    )(vectors, pair_swap(vectors, 0), pair_swap(vectors, 1))
    parts = apply(pair)
    even, odd, total = pl.pallas_call(
        functools.partial(add_kernel, rows),
        out_shape=[single, single, piece],
        in_specs=[VMEM] * rows,
        out_specs=[VMEM] * 3,
        name="add",
    )(*parts)
    first_pair, first = pl.pallas_call(
        first_kernel,
        out_shape=[pair_bf, jax.ShapeDtypeStruct((count, width), bf16)],
        in_specs=[SMEM] * 2 + [VMEM] * 4,
        out_specs=[VMEM] * 2,
        name="first",
    )(damp_center, damp_radius, pair, total, pair_swap(even, 0), pair_swap(odd, 1))
    parts = apply(first_pair)
    low, up = pl.pallas_call(
        functools.partial(add_last_kernel, rows),
        out_shape=[single, single],
        in_specs=[VMEM] * rows,
        out_specs=[VMEM] * 2,
        name="add_last",
    )(*parts)
    second = pl.pallas_call(
        second_kernel,
        out_shape=single,
        in_specs=[SMEM] * 2 + [VMEM] * 5,
        out_specs=VMEM,
        name="second",
    )(damp_center, damp_radius, vectors, first, low, pair_swap(up, 0), pair_swap(up, 1))
    return first, second


def solution(mesh):
    placed = (
        P(None, ("col", "row")),
        P(("col", "row"), None, None),
        P(("col", "row")),
        P(("col", "row")),
        P(("col", "row")),
        P(),
        P(),
    )
    return jax.shard_map(
        local,
        mesh=mesh,
        in_specs=placed,
        out_specs=(P(None, ("col", "row")), P(None, ("col", "row"))),
        check_vma=False,
    )
```

```python
import functools

import jax
import jax.numpy as jnp
from jax import lax
from jax.experimental import pallas as pl
from jax.experimental.pallas import tpu as pltpu
from jax.sharding import PartitionSpec as P

VMEM = pl.BlockSpec(memory_space=pltpu.VMEM)
SMEM = pl.BlockSpec(memory_space=pltpu.SMEM)
PARAMS = pltpu.CompilerParams(vmem_limit_bytes=12 * 1024 * 1024)
AXES = ("row", "col")


def near(array):
    return pltpu.with_memory_space_constraint(array, pltpu.VMEM)


def row_swap(block, distance):
    rows, cols = lax.axis_size("row"), lax.axis_size("col")
    route = [(r * cols + c, (r ^ distance) * cols + c) for r in range(rows) for c in range(cols)]
    return lax.ppermute(block, AXES, route)


def pair_swap(block, odd):
    rows, cols = lax.axis_size("row"), lax.axis_size("col")
    route = []
    for r in range(rows):
        for c in range(cols):
            other = c + 1 if c % 2 == odd else c - 1
            other = other if 0 <= other < cols else c
            route.append((r * cols + c, (r ^ 1) * cols + other))
    return lax.ppermute(block, AXES, route)


def load_kernel(chunk, vectors_ref, tile_ref, kept_ref, out_ref, flipped_ref, sems):
    count = tile_ref.shape[0] // chunk

    def copy(g):
        part = pl.ds(g * chunk, chunk)
        return pltpu.make_async_copy(tile_ref.at[part], out_ref.at[part], sems.at[g])

    for g in range(count):
        copy(g).start()
    kept_ref[...] = vectors_ref[...]
    for g in range(count):
        copy(g).wait()
        for k in range(g * chunk, (g + 1) * chunk):
            flipped_ref[k] = out_ref[k].T


def select_kernel(own_ref, even_ref, odd_ref, out_ref):
    col = lax.axis_index("col")
    out_ref[0] = own_ref[...]

    @pl.when(lax.rem(col, 2) == 0)
    def _():
        out_ref[1] = even_ref[...]

    @pl.when(lax.rem(col, 2) == 1)
    def _():
        inside = col < lax.axis_size("col") - 1
        out_ref[1] = jnp.where(inside, odd_ref[...], jnp.zeros_like(odd_ref))


def tiles_kernel(rows, blk, tile_row_ref, tile_offset_ref, live_ref, tile_ref, flipped_ref, *refs):
    parts = refs[:rows]
    outs = refs[rows : 2 * rows]
    window, total = refs[2 * rows :]
    span = rows * blk
    size = tile_ref.shape[-1]
    me = lax.axis_index("row")
    for s in range(rows):
        for half in range(2):
            for b in range(blk):
                window[half * span + s * blk + b] = parts[s][half, :, b * size : (b + 1) * size]
    total[...] = jnp.zeros_like(total)
    own_mask = me * blk
    next_mask = (me ^ 1) * blk
    live = live_ref[0]

    def tile(k):
        i = tile_row_ref[k]
        j = i + tile_offset_ref[k]
        at_i = i ^ own_mask
        at_j = jnp.where(j < span, j ^ own_mask, span + ((j - span) ^ next_mask))
        to_i = jnp.where(k < live, at_i, 2 * span)
        to_j = jnp.where(k < live, at_j, 2 * span)
        direct = jnp.dot(window[at_j], flipped_ref[k], preferred_element_type=jnp.float32)
        mirrored = jnp.dot(window[at_i], tile_ref[k], preferred_element_type=jnp.float32)
        return to_i, to_j, direct, mirrored

    group = 8

    def body(g, carry):
        done = [tile(g * group + k) for k in range(group)]
        for to_i, to_j, direct, mirrored in done:
            total[to_i] += direct
            total[to_j] += mirrored
        return carry

    lax.fori_loop(0, tile_ref.shape[0] // group, body, 0)
    for s in range(rows):
        for half in range(2):
            for b in range(blk):
                outs[s][half, :, b * size : (b + 1) * size] = total[half * span + s * blk + b]


def add_kernel(rows, *refs):
    parts, (even_ref, odd_ref, sum_ref) = refs[:rows], refs[rows:]
    total = parts[0][...]
    for s in range(1, rows):
        total = total + parts[s][...]
    sum_ref[...] = total
    parity = lax.rem(lax.axis_index("col"), 2)

    @pl.when(parity == 0)
    def _():
        even_ref[...] = total[1]
        odd_ref[...] = total[0]

    @pl.when(parity == 1)
    def _():
        even_ref[...] = total[0]
        odd_ref[...] = total[1]


def first_kernel(center_ref, radius_ref, vectors_ref, sum_ref, even_ref, odd_ref, out_ref, first_ref):
    col = lax.axis_index("col")
    parity = lax.rem(col, 2)
    center, radius = center_ref[0], radius_ref[0]

    def degree(image, vectors):
        return ((image - center * vectors.astype(jnp.float32)) / radius).astype(jnp.bfloat16)

    def both(from_previous, from_next):
        arrived = jnp.where(col > 0, from_previous[...], 0.0)
        own = degree(sum_ref[0] + arrived, vectors_ref[0])
        out_ref[0] = own
        first_ref[...] = own
        inside = col < lax.axis_size("col") - 1
        beyond = degree(sum_ref[1] + from_next[...], vectors_ref[1])
        out_ref[1] = jnp.where(inside, beyond, jnp.zeros_like(beyond))

    @pl.when(parity == 0)
    def _():
        both(odd_ref, even_ref)

    @pl.when(parity == 1)
    def _():
        both(even_ref, odd_ref)


def second_kernel(center_ref, radius_ref, vectors_ref, first_ref, sum_ref, even_ref, odd_ref, out_ref, first_out_ref):
    col = lax.axis_index("col")
    parity = lax.rem(col, 2)
    center, radius = center_ref[0], radius_ref[0]
    first_out_ref[...] = first_ref[...]

    def finish(from_previous):
        image = sum_ref[...] + jnp.where(col > 0, from_previous[...], 0.0)
        first = first_ref[...].astype(jnp.float32)
        out_ref[...] = 2.0 * (image - center * first) / radius - vectors_ref[...].astype(jnp.float32)

    @pl.when(parity == 0)
    def _():
        finish(odd_ref)

    @pl.when(parity == 1)
    def _():
        finish(even_ref)


def add_last_kernel(rows, *refs):
    parts, (low_ref, up_ref) = refs[:rows], refs[rows:]
    total = parts[0][...]
    for s in range(1, rows):
        total = total + parts[s][...]
    low_ref[...] = total[0]
    up_ref[...] = total[1]


def local(vectors, tile_data, tile_row, tile_offset, tile_live, damp_center, damp_radius):
    rows = lax.axis_size("row")
    count, width = vectors.shape
    size = tile_data.shape[-1]
    blk = width // size
    f32, bf16 = jnp.float32, jnp.bfloat16
    piece = pltpu.VMEM((2, count, width), f32)
    single = pltpu.VMEM((count, width), f32)
    pair_bf = pltpu.VMEM((2, count, width), bf16)
    sent = pair_swap(vectors, 0), pair_swap(vectors, 1)
    kept = pltpu.VMEM(tile_data.shape, bf16)
    chunk = 8
    vectors, tile_data, flipped = pl.pallas_call(
        functools.partial(load_kernel, chunk),
        out_shape=[pltpu.VMEM(vectors.shape, bf16), kept, kept],
        in_specs=[VMEM, pl.BlockSpec(memory_space=pltpu.HBM)],
        out_specs=[VMEM] * 3,
        scratch_shapes=[pltpu.SemaphoreType.DMA((tile_data.shape[0] // chunk,))],
        compiler_params=PARAMS,
        cost_estimate=pl.CostEstimate(
            flops=0, bytes_accessed=3 * tile_data.size * 2, transcendentals=0
        ),
        name="load",
    )(vectors, pltpu.with_memory_space_constraint(tile_data, pltpu.HBM))
    tile_data, flipped = near(tile_data), near(flipped)

    def apply(pair):
        gathered = [near(pair)] + [near(row_swap(pair, s)) for s in range(1, rows)]
        parts = pl.pallas_call(
            functools.partial(tiles_kernel, rows, blk),
            out_shape=[piece] * rows,
            in_specs=[SMEM] * 3 + [VMEM] * (2 + rows),
            out_specs=[VMEM] * rows,
            scratch_shapes=[
                pltpu.VMEM((2 * rows * blk, count, size), bf16),
                pltpu.VMEM((2 * rows * blk + 1, count, size), f32),
            ],
            compiler_params=PARAMS,
        name="tiles",
        )(tile_row, tile_offset, tile_live, tile_data, flipped, *gathered)
        return [near(parts[0])] + [near(row_swap(parts[s], s)) for s in range(1, rows)]

    pair = pl.pallas_call(
        select_kernel, out_shape=pair_bf, in_specs=[VMEM] * 3, out_specs=VMEM,
        compiler_params=PARAMS, name="select"
    )(near(vectors), near(sent[0]), near(sent[1]))
    parts = apply(pair)
    even, odd, total = pl.pallas_call(
        functools.partial(add_kernel, rows),
        out_shape=[single, single, piece],
        in_specs=[VMEM] * rows,
        out_specs=[VMEM] * 3,
        compiler_params=PARAMS,
        name="add",
    )(*parts)
    first_pair, first = pl.pallas_call(
        first_kernel,
        out_shape=[pair_bf, pltpu.VMEM((count, width), bf16)],
        in_specs=[SMEM] * 2 + [VMEM] * 4,
        out_specs=[VMEM] * 2,
        compiler_params=PARAMS,
        name="first",
    )(damp_center, damp_radius, near(pair), near(total), near(pair_swap(even, 0)), near(pair_swap(odd, 1)))
    parts = apply(first_pair)
    low, up = pl.pallas_call(
        functools.partial(add_last_kernel, rows),
        out_shape=[single, single],
        in_specs=[VMEM] * rows,
        out_specs=[VMEM] * 2,
        compiler_params=PARAMS,
        name="add_last",
    )(*parts)
    second, first = pl.pallas_call(
        second_kernel,
        out_shape=[
            jax.ShapeDtypeStruct((count, width), f32),
            jax.ShapeDtypeStruct((count, width), bf16),
        ],
        in_specs=[SMEM] * 2 + [VMEM] * 5,
        out_specs=[VMEM] * 2,
        compiler_params=PARAMS,
        name="second",
    )(damp_center, damp_radius, near(vectors), near(first), near(low), near(pair_swap(up, 0)), near(pair_swap(up, 1)))
    return first, second


def solution(mesh):
    placed = (
        P(None, ("col", "row")),
        P(("col", "row"), None, None),
        P(("col", "row")),
        P(("col", "row")),
        P(("col", "row")),
        P(),
        P(),
    )
    return jax.shard_map(
        local,
        mesh=mesh,
        in_specs=placed,
        out_specs=(P(None, ("col", "row")), P(None, ("col", "row"))),
        check_vma=False,
    )
```

```python
import functools

import jax
import jax.numpy as jnp
from jax import lax
from jax.experimental import pallas as pl
from jax.experimental.pallas import tpu as pltpu
from jax.sharding import PartitionSpec as P

VMEM = pl.BlockSpec(memory_space=pltpu.VMEM)
SMEM = pl.BlockSpec(memory_space=pltpu.SMEM)
HBM = pl.BlockSpec(memory_space=pltpu.HBM)
AXES = ("row", "col")
F32, BF16 = jnp.float32, jnp.bfloat16


def call(kernel, name, outs, places, args, scratch=(), cost=None):
    spaces = {id(VMEM): pltpu.VMEM, id(HBM): pltpu.HBM}
    args = [
        pltpu.with_memory_space_constraint(a, spaces[id(p)]) if id(p) in spaces else a
        for a, p in zip(args, places)
    ]
    results = pl.pallas_call(
        kernel,
        out_shape=list(outs),
        in_specs=list(places),
        out_specs=[VMEM] * len(outs),
        scratch_shapes=list(scratch),
        compiler_params=pltpu.CompilerParams(vmem_limit_bytes=12 * 1024 * 1024),
        cost_estimate=cost,
        name=name,
    )(*args)
    return list(results)


def row_swap(block, distance):
    rows, cols = lax.axis_size("row"), lax.axis_size("col")
    route = [(r * cols + c, (r ^ distance) * cols + c) for r in range(rows) for c in range(cols)]
    return lax.ppermute(block, AXES, route)


def pair_swap(block, odd):
    rows, cols = lax.axis_size("row"), lax.axis_size("col")
    route = []
    for r in range(rows):
        for c in range(cols):
            other = c + 1 if c % 2 == odd else c - 1
            other = other if 0 <= other < cols else c
            route.append((r * cols + c, (r ^ 1) * cols + other))
    return lax.ppermute(block, AXES, route)


def by_parity(even_case, odd_case):
    parity = lax.rem(lax.axis_index("col"), 2)
    pl.when(parity == 0)(even_case)
    pl.when(parity == 1)(odd_case)


def load_kernel(chunk, span, blk, row_hbm, offset_hbm, vectors_hbm, tile_hbm, *refs):
    kept_ref, out_ref, flipped_ref, index_ref, row_ref, offset_ref, sems = refs
    count = tile_hbm.shape[0] // chunk
    small = [
        pltpu.make_async_copy(source, target, sems.at[count + n])
        for n, (source, target) in enumerate(
            [
                (row_hbm, row_ref),
                (offset_hbm, offset_ref),
                (vectors_hbm, kept_ref),
            ]
        )
    ]

    def copy(g):
        part = pl.ds(g * chunk, chunk)
        return pltpu.make_async_copy(tile_hbm.at[part], out_ref.at[part], sems.at[g])

    for one in small:
        one.start()
    for g in range(count):
        copy(g).start()
    for one in small:
        one.wait()
    me = lax.axis_index("row")
    i = row_ref[...]
    j = i + offset_ref[...]
    at_i = i ^ (me * blk)
    at_j = jnp.where(j < span, j ^ (me * blk), span + ((j - span) ^ ((me ^ 1) * blk)))
    index_ref[0:1] = at_i
    index_ref[1:2] = at_j
    for g in range(count):
        copy(g).wait()
        for k in range(g * chunk, (g + 1) * chunk):
            flipped_ref[k] = out_ref[k].T


def select_kernel(own_ref, even_ref, odd_ref, out_ref):
    col = lax.axis_index("col")
    size = out_ref.shape[-1]

    def split(half, value):
        for b in range(out_ref.shape[1]):
            out_ref[half, b] = value[:, b * size : (b + 1) * size]

    split(0, own_ref[...])

    def even_case():
        split(1, even_ref[...])

    def odd_case():
        inside = col < lax.axis_size("col") - 1
        split(1, jnp.where(inside, odd_ref[...], jnp.zeros_like(odd_ref)))

    by_parity(even_case, odd_case)


def tiles_kernel(slots, evens, live_ref, index_ref, tile_ref, flipped_ref, *refs):
    parts = refs[: len(slots)]
    keep_ref, send_ref, window, total = refs[len(slots) :]
    blk = keep_ref.shape[2]
    span = (window.shape[0]) // 2
    for part, wanted in zip(parts, slots):
        for half in range(2):
            for n, s in enumerate(wanted):
                for b in range(blk):
                    value = part[half, n, b] if len(part.shape) == 5 else part[half, b]
                    window[half * span + s * blk + b] = value
    total[...] = jnp.zeros_like(total)
    for k in range(tile_ref.shape[0]):
        direct = jnp.dot(window[index_ref[1, k]], flipped_ref[k], preferred_element_type=F32)
        mirrored = jnp.dot(window[index_ref[0, k]], tile_ref[k], preferred_element_type=F32)
        live = k < live_ref[0]
        total[jnp.where(live, index_ref[0, k], 2 * span)] += direct
        total[jnp.where(live, index_ref[1, k], 2 * span)] += mirrored
    for half in range(2):
        for n, s in enumerate(evens):
            for b in range(blk):
                keep_ref[half, n, b] = total[half * span + s * blk + b]
                send_ref[half, n, b] = total[half * span + (s ^ 1) * blk + b]


def add_kernel(keep_ref, got_ref, out_ref):
    out_ref[...] = keep_ref[...] + got_ref[...]


def gather_kernel(evens, own_ref, *refs):
    others, (even_ref, odd_ref, sum_ref) = refs[: len(evens) - 1], refs[len(evens) - 1 :]
    place = {s: n for n, s in enumerate(evens)}
    for n, s in enumerate(evens):
        value = own_ref[:, n]
        for other, g in zip(others, evens[1:]):
            value = value + other[:, place[s ^ g]]
        sum_ref[:, n] = value

    def even_case():
        even_ref[...] = sum_ref[1]
        odd_ref[...] = sum_ref[0]

    def odd_case():
        even_ref[...] = sum_ref[0]
        odd_ref[...] = sum_ref[1]

    by_parity(even_case, odd_case)


def first_kernel(evens, center_ref, radius_ref, sum_ref, even_ref, odd_ref, *refs):
    parts, out_ref = refs[:-1], refs[-1]
    col = lax.axis_index("col")
    center, radius = center_ref[0], radius_ref[0]

    def degree(image, vectors):
        return ((image - center * vectors.astype(F32)) / radius).astype(BF16)

    def both(from_previous, from_next):
        inside = col < lax.axis_size("col") - 1
        for n in range(len(evens)):
            arrived = jnp.where(col > 0, from_previous[n], 0.0)
            out_ref[0, n] = degree(sum_ref[0, n] + arrived, parts[n][0])
            beyond = degree(sum_ref[1, n] + from_next[n], parts[n][1])
            out_ref[1, n] = jnp.where(inside, beyond, jnp.zeros_like(beyond))

    by_parity(lambda: both(odd_ref, even_ref), lambda: both(even_ref, odd_ref))


def spread_kernel(keep_ref, got_ref, *outs):
    for n, out_ref in enumerate(outs):
        out_ref[...] = keep_ref[:, n] + got_ref[:, n]


def owner_kernel(count, *refs):
    parts, (low_ref, up_ref) = refs[:count], refs[count:]
    low, up = parts[0][0], parts[0][1]
    for part in parts[1:]:
        low, up = low + part[0], up + part[1]
    low_ref[...] = low
    up_ref[...] = up


def second_kernel(center_ref, radius_ref, pair_ref, first_ref, low_ref, even_ref, odd_ref, out_ref, first_out_ref):
    col = lax.axis_index("col")
    center, radius = center_ref[0], radius_ref[0]
    size = low_ref.shape[-1]

    def finish(from_previous):
        for b in range(low_ref.shape[0]):
            image = low_ref[b] + jnp.where(col > 0, from_previous[b], 0.0)
            first = first_ref[0, 0, b].astype(F32)
            second = 2.0 * (image - center * first) / radius - pair_ref[0, b].astype(F32)
            out_ref[:, b * size : (b + 1) * size] = second

    for b in range(low_ref.shape[0]):
        first_out_ref[:, b * size : (b + 1) * size] = first_ref[0, 0, b]
    by_parity(lambda: finish(odd_ref), lambda: finish(even_ref))


def local(vectors, tile_data, tile_row, tile_offset, tile_live, damp_center, damp_radius):
    rows = lax.axis_size("row")
    count, width = vectors.shape
    tiles, size, _ = tile_data.shape
    blk = width // size
    span = rows * blk
    evens = [s for s in range(rows) if bin(s).count("1") % 2 == 0]
    members = len(evens)

    def shape(dtype, *lead):
        return pltpu.VMEM((*lead, count, size), dtype)

    sent = pair_swap(vectors, 0), pair_swap(vectors, 1)
    kept = pltpu.VMEM(tile_data.shape, BF16)
    chunk = 8
    vectors, tile_data, flipped, index = call(
        functools.partial(load_kernel, chunk, span, blk),
        "load",
        [pltpu.VMEM(vectors.shape, BF16), kept, kept, pltpu.VMEM((2, tiles), jnp.int32)],
        [HBM] * 4,
        [tile_row.reshape(1, tiles), tile_offset.reshape(1, tiles), vectors, tile_data],
        scratch=[
            pltpu.VMEM((1, tiles), jnp.int32),
            pltpu.VMEM((1, tiles), jnp.int32),
            pltpu.SemaphoreType.DMA((tiles // chunk + 3,)),
        ],
        cost=pl.CostEstimate(flops=0, bytes_accessed=6 * tile_data.size, transcendentals=0),
    )

    def apply(parts, slots):
        index_near = pltpu.with_memory_space_constraint(index, pltpu.VMEM)
        keep, send = call(
            functools.partial(tiles_kernel, slots, evens),
            "tiles",
            [shape(F32, 2, members, blk)] * 2,
            [SMEM] * 2 + [VMEM] * (2 + len(parts)),
            [tile_live, index_near, tile_data, flipped, *parts],
            scratch=[
                pltpu.VMEM((2 * span, count, size), BF16),
                pltpu.VMEM((2 * span + 1, count, size), F32),
            ],
        )
        return keep, row_swap(send, 1)

    (pair,) = call(select_kernel, "select", [shape(BF16, 2, blk)], [VMEM] * 3, [vectors, *sent])
    gathered = [pair] + [row_swap(pair, s) for s in range(1, rows)]
    keep, got = apply(gathered, [[s] for s in range(rows)])
    (paired,) = call(add_kernel, "add", [shape(F32, 2, members, blk)], [VMEM] * 2, [keep, got])
    even, odd, total = call(
        functools.partial(gather_kernel, evens),
        "gather",
        [shape(F32, members, blk)] * 2 + [shape(F32, 2, members, blk)],
        [VMEM] * members,
        [paired] + [row_swap(paired, g) for g in evens[1:]],
    )
    (first,) = call(
        functools.partial(first_kernel, evens),
        "first",
        [shape(BF16, 2, members, blk)],
        [SMEM] * 2 + [VMEM] * (3 + members),
        [damp_center, damp_radius, total, pair_swap(even, 0), pair_swap(odd, 1)]
        + [gathered[s] for s in evens],
    )
    keep, got = apply([first, row_swap(first, 1)], [evens, [s ^ 1 for s in evens]])
    pieces = call(spread_kernel, "spread", [shape(F32, 2, blk)] * members, [VMEM] * 2, [keep, got])
    pieces = pieces[:1] + [row_swap(p, g) for p, g in zip(pieces[1:], evens[1:])]
    low, up = call(
        functools.partial(owner_kernel, members), "owner", [shape(F32, blk)] * 2, [VMEM] * members, pieces
    )
    second, first = call(
        second_kernel,
        "second",
        [jax.ShapeDtypeStruct((count, width), F32), jax.ShapeDtypeStruct((count, width), BF16)],
        [SMEM] * 2 + [VMEM] * 5,
        [damp_center, damp_radius, pair, first, low, pair_swap(up, 0), pair_swap(up, 1)],
    )
    return first, second


def solution(mesh):
    placed = (
        P(None, ("col", "row")),
        P(("col", "row"), None, None),
        P(("col", "row")),
        P(("col", "row")),
        P(("col", "row")),
        P(),
        P(),
    )
    return jax.shard_map(
        local,
        mesh=mesh,
        in_specs=placed,
        out_specs=(P(None, ("col", "row")), P(None, ("col", "row"))),
        check_vma=False,
    )
```

```python
import functools

import jax
import jax.numpy as jnp
from jax import lax
from jax.experimental import pallas as pl
from jax.experimental.pallas import tpu as pltpu
from jax.sharding import PartitionSpec as P

VMEM = pl.BlockSpec(memory_space=pltpu.VMEM)
SMEM = pl.BlockSpec(memory_space=pltpu.SMEM)
HBM = pl.BlockSpec(memory_space=pltpu.HBM)
AXES = ("row", "col")
F32, BF16 = jnp.float32, jnp.bfloat16


def call(kernel, name, outs, places, args, scratch=(), cost=None):
    spaces = {id(VMEM): pltpu.VMEM, id(HBM): pltpu.HBM}
    args = [
        pltpu.with_memory_space_constraint(a, spaces[id(p)]) if id(p) in spaces else a
        for a, p in zip(args, places)
    ]
    results = pl.pallas_call(
        kernel,
        out_shape=list(outs),
        in_specs=list(places),
        out_specs=[SMEM if getattr(o, "memory_space", None) == pltpu.SMEM else VMEM for o in outs],
        scratch_shapes=list(scratch),
        compiler_params=pltpu.CompilerParams(vmem_limit_bytes=12 * 1024 * 1024),
        cost_estimate=cost,
        name=name,
    )(*args)
    return list(results)


def row_swap(block, distance):
    rows, cols = lax.axis_size("row"), lax.axis_size("col")
    route = [(r * cols + c, (r ^ distance) * cols + c) for r in range(rows) for c in range(cols)]
    return lax.ppermute(block, AXES, route)


def pair_swap(block, odd):
    rows, cols = lax.axis_size("row"), lax.axis_size("col")
    route = []
    for r in range(rows):
        for c in range(cols):
            other = c + 1 if c % 2 == odd else c - 1
            other = other if 0 <= other < cols else c
            route.append((r * cols + c, (r ^ 1) * cols + other))
    return lax.ppermute(block, AXES, route)


def by_parity(even_case, odd_case):
    parity = lax.rem(lax.axis_index("col"), 2)
    pl.when(parity == 0)(even_case)
    pl.when(parity == 1)(odd_case)


def load_kernel(chunk, span, blk, row_hbm, offset_hbm, vectors_hbm, tile_hbm, *refs):
    kept_ref, out_ref, flipped_ref, index_ref, row_ref, offset_ref, sems = refs
    count = tile_hbm.shape[0] // chunk
    small = [
        pltpu.make_async_copy(source, target, sems.at[count + n])
        for n, (source, target) in enumerate(
            [
                (row_hbm, row_ref),
                (offset_hbm, offset_ref),
                (vectors_hbm, kept_ref),
            ]
        )
    ]

    def copy(g):
        part = pl.ds(g * chunk, chunk)
        return pltpu.make_async_copy(tile_hbm.at[part], out_ref.at[part], sems.at[g])

    for one in small:
        one.start()
    for g in range(count):
        copy(g).start()
    for one in small:
        one.wait()
    me = lax.axis_index("row")
    for k in range(tile_hbm.shape[0]):
        i = row_ref[0, k]
        j = i + offset_ref[0, k]
        index_ref[0, k] = i ^ (me * blk)
        index_ref[1, k] = jnp.where(j < span, j ^ (me * blk), span + ((j - span) ^ ((me ^ 1) * blk)))
    for g in range(count):
        copy(g).wait()
        for k in range(g * chunk, (g + 1) * chunk):
            flipped_ref[k] = out_ref[k].T


def select_kernel(own_ref, even_ref, odd_ref, out_ref):
    col = lax.axis_index("col")
    size = out_ref.shape[-1]

    def lay(half, value):
        for b in range(out_ref.shape[1]):
            out_ref[half, b] = value[:, b * size : (b + 1) * size]

    lay(0, own_ref[...])

    def even_case():
        lay(1, even_ref[...])

    def odd_case():
        inside = col < lax.axis_size("col") - 1
        lay(1, jnp.where(inside, odd_ref[...], jnp.zeros_like(odd_ref)))

    by_parity(even_case, odd_case)


def fill(window, half, parts, slots):
    for part, wanted in zip(parts, slots):
        for n, s in enumerate(wanted):
            blk = part.shape[-3]
            for b in range(blk):
                value = part[half, n, b] if len(part.shape) == 5 else part[half, b]
                window[s * blk + b] = value


def split(total, first, evens, keep_ref, send_ref):
    blk = keep_ref.shape[1]
    for n, s in enumerate(evens):
        for b in range(blk):
            keep_ref[n, b] = total[first + s * blk + b]
            send_ref[n, b] = total[first + (s ^ 1) * blk + b]


def mirror_kernel(slots, evens, live_ref, index_ref, tile_ref, *refs):
    parts = refs[: len(slots)]
    keep_ref, send_ref, low_ref, window, total = refs[len(slots) :]
    span = window.shape[0]
    fill(window, 0, parts, slots)
    total[...] = jnp.zeros_like(total)
    for k in range(tile_ref.shape[0]):
        mirrored = jnp.dot(window[index_ref[0, k]], tile_ref[k], preferred_element_type=F32)
        total[jnp.where(k < live_ref[0], index_ref[1, k], 2 * span)] += mirrored
    split(total, span, evens, keep_ref, send_ref)
    low_ref[...] = total[0:span]


def direct_kernel(slots, evens, live_ref, index_ref, flipped_ref, low_ref, *refs):
    parts = refs[: len(slots)]
    keep_ref, send_ref, window, total = refs[len(slots) :]
    span = low_ref.shape[0]
    for half in range(2):
        fill(window.at[half * span : (half + 1) * span], half, parts, slots)
    total[0:span] = low_ref[...]
    total[span] = jnp.zeros(total.shape[1:], F32)
    for k in range(flipped_ref.shape[0]):
        direct = jnp.dot(window[index_ref[1, k]], flipped_ref[k], preferred_element_type=F32)
        total[jnp.where(k < live_ref[0], index_ref[0, k], span)] += direct
    split(total, 0, evens, keep_ref, send_ref)


def add_kernel(keep_ref, got_ref, out_ref):
    out_ref[...] = keep_ref[...] + got_ref[...]


def gather_kernel(evens, *refs):
    members = len(evens)
    halves = refs[:members], refs[members : 2 * members]
    even_ref, odd_ref, sum_ref = refs[2 * members :]
    place = {s: n for n, s in enumerate(evens)}
    for half, (own_ref, *others) in enumerate(halves):
        for n, s in enumerate(evens):
            value = own_ref[n]
            for other, g in zip(others, evens[1:]):
                value = value + other[place[s ^ g]]
            sum_ref[half, n] = value

    def even_case():
        even_ref[...] = sum_ref[1]
        odd_ref[...] = sum_ref[0]

    def odd_case():
        even_ref[...] = sum_ref[0]
        odd_ref[...] = sum_ref[1]

    by_parity(even_case, odd_case)


def first_kernel(evens, center_ref, radius_ref, sum_ref, odd_ref, even_ref, *refs):
    parts, out_ref = refs[:-1], refs[-1]
    col = lax.axis_index("col")
    center, radius = center_ref[0], radius_ref[0]

    def degree(image, vectors):
        return ((image - center * vectors.astype(F32)) / radius).astype(BF16)

    def both(from_previous, from_next):
        inside = col < lax.axis_size("col") - 1
        for n in range(len(evens)):
            arrived = jnp.where(col > 0, from_previous[n], 0.0)
            out_ref[0, n] = degree(sum_ref[0, n] + arrived, parts[n][0])
            beyond = degree(sum_ref[1, n] + from_next[n], parts[n][1])
            out_ref[1, n] = jnp.where(inside, beyond, jnp.zeros_like(beyond))

    by_parity(lambda: both(odd_ref, even_ref), lambda: both(even_ref, odd_ref))


def spread_kernel(keep_ref, got_ref, *outs):
    for n, out_ref in enumerate(outs):
        out_ref[...] = keep_ref[n] + got_ref[n]


def owner_kernel(*refs):
    parts, out_ref = refs[:-1], refs[-1]
    total = parts[0][...]
    for part in parts[1:]:
        total = total + part[...]
    out_ref[...] = total


def second_kernel(center_ref, radius_ref, pair_ref, first_ref, even_ref, odd_ref, *refs):
    parts, (out_ref, first_out_ref) = refs[:-2], refs[-2:]
    col = lax.axis_index("col")
    center, radius = center_ref[0], radius_ref[0]
    blk, _, size = even_ref.shape

    def finish(from_previous):
        for b in range(blk):
            image = jnp.where(col > 0, from_previous[b], 0.0)
            for part in parts:
                image = image + part[b]
            first = first_ref[0, 0, b].astype(F32)
            second = 2.0 * (image - center * first) / radius - pair_ref[0, b].astype(F32)
            out_ref[:, b * size : (b + 1) * size] = second

    for b in range(blk):
        first_out_ref[:, b * size : (b + 1) * size] = first_ref[0, 0, b]
    by_parity(lambda: finish(odd_ref), lambda: finish(even_ref))


def local(vectors, tile_data, tile_row, tile_offset, tile_live, damp_center, damp_radius):
    rows = lax.axis_size("row")
    count, width = vectors.shape
    tiles, size, _ = tile_data.shape
    blk = width // size
    span = rows * blk
    evens = [s for s in range(rows) if bin(s).count("1") % 2 == 0]
    members = len(evens)

    def shape(dtype, *lead):
        return pltpu.VMEM((*lead, count, size), dtype)

    sent = pair_swap(vectors, 0), pair_swap(vectors, 1)
    kept = pltpu.VMEM(tile_data.shape, BF16)
    chunk = 8
    vectors, tile_data, flipped, index = call(
        functools.partial(load_kernel, chunk, span, blk),
        "load",
        [pltpu.VMEM(vectors.shape, BF16), kept, kept, pltpu.SMEM((2, tiles), jnp.int32)],
        [HBM] * 4,
        [tile_row.reshape(1, tiles), tile_offset.reshape(1, tiles), vectors, tile_data],
        scratch=[
            pltpu.SMEM((1, tiles), jnp.int32),
            pltpu.SMEM((1, tiles), jnp.int32),
            pltpu.SemaphoreType.DMA((tiles // chunk + 3,)),
        ],
        cost=pl.CostEstimate(flops=0, bytes_accessed=6 * tile_data.size, transcendentals=0),
    )

    flops = 2 * tiles * count * size * size
    cost = pl.CostEstimate(flops=flops, bytes_accessed=2 * tile_data.size, transcendentals=0)

    def apply(parts, slots):
        half = shape(F32, members, blk)
        keep_up, send_up, low = call(
            functools.partial(mirror_kernel, slots, evens),
            "mirror",
            [half, half, shape(F32, span)],
            [SMEM] * 2 + [VMEM] * (1 + len(parts)),
            [tile_live, index, tile_data, *parts],
            scratch=[
                pltpu.VMEM((span, count, size), BF16),
                pltpu.VMEM((2 * span + 1, count, size), F32),
            ],
            cost=cost,
        )
        got_up = row_swap(send_up, 1)
        keep_low, send_low = call(
            functools.partial(direct_kernel, slots, evens),
            "direct",
            [half, half],
            [SMEM] * 2 + [VMEM] * (2 + len(parts)),
            [tile_live, index, flipped, low, *parts],
            scratch=[
                pltpu.VMEM((2 * span, count, size), BF16),
                pltpu.VMEM((span + 1, count, size), F32),
            ],
            cost=cost,
        )
        return (keep_up, got_up), (keep_low, row_swap(send_low, 1))

    (pair,) = call(select_kernel, "select", [shape(BF16, 2, blk)], [VMEM] * 3, [vectors, *sent])
    gathered = [pair] + [row_swap(pair, s) for s in range(1, rows)]
    up, low = apply(gathered, [[s] for s in range(rows)])

    def pair_sum(ours):
        (paired,) = call(add_kernel, "add", [shape(F32, members, blk)], [VMEM] * 2, ours)
        return [paired] + [row_swap(paired, g) for g in evens[1:]]

    up = pair_sum(up)
    low = pair_sum(low)
    even, odd, total = call(
        functools.partial(gather_kernel, evens),
        "gather",
        [shape(F32, members, blk)] * 2 + [shape(F32, 2, members, blk)],
        [VMEM] * (2 * members),
        low + up,
    )
    (first,) = call(
        functools.partial(first_kernel, evens),
        "first",
        [shape(BF16, 2, members, blk)],
        [SMEM] * 2 + [VMEM] * (3 + members),
        [damp_center, damp_radius, total, pair_swap(odd, 1), pair_swap(even, 0)]
        + [gathered[s] for s in evens],
    )
    up, low = apply([first, row_swap(first, 1)], [evens, [s ^ 1 for s in evens]])

    def pieces(ours):
        parts = call(spread_kernel, "spread", [shape(F32, blk)] * members, [VMEM] * 2, ours)
        return parts[:1] + [row_swap(p, g) for p, g in zip(parts[1:], evens[1:])]

    up = pieces(up)
    low = pieces(low)
    (up,) = call(owner_kernel, "owner", [shape(F32, blk)], [VMEM] * members, up)
    second, first = call(
        second_kernel,
        "second",
        [jax.ShapeDtypeStruct((count, width), F32), jax.ShapeDtypeStruct((count, width), BF16)],
        [SMEM] * 2 + [VMEM] * (4 + members),
        [damp_center, damp_radius, pair, first, pair_swap(up, 0), pair_swap(up, 1), *low],
    )
    return first, second


def solution(mesh):
    placed = (
        P(None, ("col", "row")),
        P(("col", "row"), None, None),
        P(("col", "row")),
        P(("col", "row")),
        P(("col", "row")),
        P(),
        P(),
    )
    return jax.shard_map(
        local,
        mesh=mesh,
        in_specs=placed,
        out_specs=(P(None, ("col", "row")), P(None, ("col", "row"))),
        check_vma=False,
    )
```

```python
import functools

import jax
import jax.numpy as jnp
from jax import lax
from jax.experimental import pallas as pl
from jax.experimental.pallas import tpu as pltpu
from jax.sharding import PartitionSpec as P

VMEM = pl.BlockSpec(memory_space=pltpu.VMEM)
SMEM = pl.BlockSpec(memory_space=pltpu.SMEM)
HBM = pl.BlockSpec(memory_space=pltpu.HBM)
AXES = ("row", "col")
F32, BF16 = jnp.float32, jnp.bfloat16


def call(kernel, name, outs, places, args, scratch=(), cost=None):
    spaces = {id(VMEM): pltpu.VMEM, id(HBM): pltpu.HBM}
    args = [
        pltpu.with_memory_space_constraint(a, spaces[id(p)]) if id(p) in spaces else a
        for a, p in zip(args, places)
    ]
    results = pl.pallas_call(
        kernel,
        out_shape=list(outs),
        in_specs=list(places),
        out_specs=[SMEM if getattr(o, "memory_space", None) == pltpu.SMEM else VMEM for o in outs],
        scratch_shapes=list(scratch),
        compiler_params=pltpu.CompilerParams(vmem_limit_bytes=12 * 1024 * 1024),
        cost_estimate=cost,
        name=name,
    )(*args)
    return list(results)


def row_swap(block, distance):
    rows, cols = lax.axis_size("row"), lax.axis_size("col")
    route = [(r * cols + c, (r ^ distance) * cols + c) for r in range(rows) for c in range(cols)]
    return lax.ppermute(block, AXES, route)


def pair_swap(block, odd):
    rows, cols = lax.axis_size("row"), lax.axis_size("col")
    route = []
    for r in range(rows):
        for c in range(cols):
            other = c + 1 if c % 2 == odd else c - 1
            other = other if 0 <= other < cols else c
            route.append((r * cols + c, (r ^ 1) * cols + other))
    return lax.ppermute(block, AXES, route)


def by_parity(even_case, odd_case):
    parity = lax.rem(lax.axis_index("col"), 2)
    pl.when(parity == 0)(even_case)
    pl.when(parity == 1)(odd_case)


def encode(blocks, out_ref):
    most = jnp.abs(blocks[0])
    for block in blocks[1:]:
        most = jnp.maximum(most, jnp.abs(block))
    most = jnp.broadcast_to(jnp.max(most, axis=1, keepdims=True), most.shape)
    exponent = jnp.ceil(jnp.log2(jnp.maximum(most, 1e-30)))
    scale = jnp.exp2(-exponent) * 32767.0
    for n, block in enumerate(blocks):
        code = jnp.clip(jnp.round(block * scale), -32767.0, 32767.0)
        out_ref[n] = code.astype(jnp.int32).astype(jnp.int16)
    out_ref[len(blocks)] = exponent.astype(jnp.int32).astype(jnp.int16)


def step_of(code_ref):
    exponent = code_ref[code_ref.shape[0] - 1].astype(jnp.int32).astype(F32)
    return jnp.exp2(exponent) * (1.0 / 32767.0)


def decode(code_ref, n, step):
    return code_ref[n].astype(jnp.int32).astype(F32) * step


def load_kernel(chunk, span, blk, row_hbm, offset_hbm, vectors_hbm, tile_hbm, *refs):
    kept_ref, out_ref, flipped_ref, index_ref, row_ref, offset_ref, sems = refs
    count = tile_hbm.shape[0] // chunk
    small = [
        pltpu.make_async_copy(source, target, sems.at[count + n])
        for n, (source, target) in enumerate(
            [
                (row_hbm, row_ref),
                (offset_hbm, offset_ref),
                (vectors_hbm, kept_ref),
            ]
        )
    ]

    def copy(g):
        part = pl.ds(g * chunk, chunk)
        return pltpu.make_async_copy(tile_hbm.at[part], out_ref.at[part], sems.at[g])

    for one in small:
        one.start()
    for g in range(count):
        copy(g).start()
    for one in small:
        one.wait()
    me = lax.axis_index("row")
    for k in range(tile_hbm.shape[0]):
        i = row_ref[0, k]
        j = i + offset_ref[0, k]
        index_ref[0, k] = i ^ (me * blk)
        index_ref[1, k] = jnp.where(j < span, j ^ (me * blk), span + ((j - span) ^ ((me ^ 1) * blk)))
    for g in range(count):
        copy(g).wait()
        for k in range(g * chunk, (g + 1) * chunk):
            flipped_ref[k] = out_ref[k].T


def select_kernel(own_ref, even_ref, odd_ref, out_ref):
    col = lax.axis_index("col")
    size = out_ref.shape[-1]

    def lay(half, value):
        for b in range(out_ref.shape[1]):
            out_ref[half, b] = value[:, b * size : (b + 1) * size]

    lay(0, own_ref[...])

    def even_case():
        lay(1, even_ref[...])

    def odd_case():
        inside = col < lax.axis_size("col") - 1
        lay(1, jnp.where(inside, odd_ref[...], jnp.zeros_like(odd_ref)))

    by_parity(even_case, odd_case)


def fill(window, half, parts, slots):
    for part, wanted in zip(parts, slots):
        for n, s in enumerate(wanted):
            blk = part.shape[-3]
            for b in range(blk):
                value = part[half, n, b] if len(part.shape) == 5 else part[half, b]
                window[s * blk + b] = value


def split(total, first, evens, keep_ref, send_ref):
    blk = keep_ref.shape[1]
    for n, s in enumerate(evens):
        for b in range(blk):
            keep_ref[n, b] = total[first + s * blk + b]
            send_ref[n, b] = total[first + (s ^ 1) * blk + b]


def mirror_kernel(slots, evens, live_ref, index_ref, tile_ref, *refs):
    parts = refs[: len(slots)]
    keep_ref, send_ref, low_ref, window, total = refs[len(slots) :]
    span = window.shape[0]
    fill(window, 0, parts, slots)
    total[...] = jnp.zeros_like(total)
    for k in range(tile_ref.shape[0]):
        mirrored = jnp.dot(window[index_ref[0, k]], tile_ref[k], preferred_element_type=F32)
        total[jnp.where(k < live_ref[0], index_ref[1, k], 2 * span)] += mirrored
    split(total, span, evens, keep_ref, send_ref)
    low_ref[...] = total[0:span]


def direct_kernel(slots, evens, live_ref, index_ref, flipped_ref, low_ref, *refs):
    parts = refs[: len(slots)]
    keep_ref, send_ref, window, total = refs[len(slots) :]
    span = low_ref.shape[0]
    for half in range(2):
        fill(window.at[half * span : (half + 1) * span], half, parts, slots)
    total[0:span] = low_ref[...]
    total[span] = jnp.zeros(total.shape[1:], F32)
    for k in range(flipped_ref.shape[0]):
        direct = jnp.dot(window[index_ref[1, k]], flipped_ref[k], preferred_element_type=F32)
        total[jnp.where(k < live_ref[0], index_ref[0, k], span)] += direct
    split(total, 0, evens, keep_ref, send_ref)


def add_kernel(keep_ref, got_ref, out_ref, code_ref):
    members, blk = out_ref.shape[:2]
    out_ref[...] = keep_ref[...] + got_ref[...]
    encode([out_ref[n, b] for n in range(members) for b in range(blk)], code_ref)


def gather_kernel(evens, *refs):
    members = len(evens)
    halves = refs[:members], refs[members : 2 * members]
    even_ref, odd_ref, sum_ref = refs[2 * members :]
    blk = sum_ref.shape[2]
    place = {s: n for n, s in enumerate(evens)}
    for half, (own_ref, *others) in enumerate(halves):
        steps = [step_of(other) for other in others]
        for n, s in enumerate(evens):
            for b in range(blk):
                value = own_ref[n, b]
                for other, step, g in zip(others, steps, evens[1:]):
                    value = value + decode(other, place[s ^ g] * blk + b, step)
                sum_ref[half, n, b] = value

    def code(half, out_ref):
        encode([sum_ref[half, n, b] for n in range(members) for b in range(blk)], out_ref)

    def even_case():
        code(1, even_ref)
        code(0, odd_ref)

    def odd_case():
        code(0, even_ref)
        code(1, odd_ref)

    by_parity(even_case, odd_case)


def first_kernel(evens, center_ref, radius_ref, sum_ref, odd_ref, even_ref, *refs):
    parts, out_ref = refs[:-1], refs[-1]
    col = lax.axis_index("col")
    center, radius = center_ref[0], radius_ref[0]

    def degree(image, vectors):
        return ((image - center * vectors.astype(F32)) / radius).astype(BF16)

    def both(from_previous, from_next):
        inside = col < lax.axis_size("col") - 1
        blk = out_ref.shape[2]
        previous_step, next_step = step_of(from_previous), step_of(from_next)
        for n in range(len(evens)):
            for b in range(blk):
                arrived = decode(from_previous, n * blk + b, previous_step)
                arrived = jnp.where(col > 0, arrived, 0.0)
                out_ref[0, n, b] = degree(sum_ref[0, n, b] + arrived, parts[n][0, b])
                arrived = decode(from_next, n * blk + b, next_step)
                beyond = degree(sum_ref[1, n, b] + arrived, parts[n][1, b])
                out_ref[1, n, b] = jnp.where(inside, beyond, jnp.zeros_like(beyond))

    by_parity(lambda: both(odd_ref, even_ref), lambda: both(even_ref, odd_ref))


def spread_kernel(keep_ref, got_ref, *outs):
    for n, out_ref in enumerate(outs):
        out_ref[...] = keep_ref[n] + got_ref[n]


def owner_kernel(*refs):
    parts, out_ref = refs[:-1], refs[-1]
    total = parts[0][...]
    for part in parts[1:]:
        total = total + part[...]
    out_ref[...] = total


def second_kernel(center_ref, radius_ref, pair_ref, first_ref, even_ref, odd_ref, *refs):
    parts, (out_ref, first_out_ref) = refs[:-2], refs[-2:]
    col = lax.axis_index("col")
    center, radius = center_ref[0], radius_ref[0]
    blk, _, size = even_ref.shape

    def finish(from_previous):
        for b in range(blk):
            image = jnp.where(col > 0, from_previous[b], 0.0)
            for part in parts:
                image = image + part[b]
            first = first_ref[0, 0, b].astype(F32)
            second = 2.0 * (image - center * first) / radius - pair_ref[0, b].astype(F32)
            out_ref[:, b * size : (b + 1) * size] = second

    for b in range(blk):
        first_out_ref[:, b * size : (b + 1) * size] = first_ref[0, 0, b]
    by_parity(lambda: finish(odd_ref), lambda: finish(even_ref))


def local(vectors, tile_data, tile_row, tile_offset, tile_live, damp_center, damp_radius):
    rows = lax.axis_size("row")
    count, width = vectors.shape
    tiles, size, _ = tile_data.shape
    blk = width // size
    span = rows * blk
    evens = [s for s in range(rows) if bin(s).count("1") % 2 == 0]
    members = len(evens)

    def shape(dtype, *lead):
        return pltpu.VMEM((*lead, count, size), dtype)

    sent = pair_swap(vectors, 0), pair_swap(vectors, 1)
    kept = pltpu.VMEM(tile_data.shape, BF16)
    chunk = 8
    vectors, tile_data, flipped, index = call(
        functools.partial(load_kernel, chunk, span, blk),
        "load",
        [pltpu.VMEM(vectors.shape, BF16), kept, kept, pltpu.SMEM((2, tiles), jnp.int32)],
        [HBM] * 4,
        [tile_row.reshape(1, tiles), tile_offset.reshape(1, tiles), vectors, tile_data],
        scratch=[
            pltpu.SMEM((1, tiles), jnp.int32),
            pltpu.SMEM((1, tiles), jnp.int32),
            pltpu.SemaphoreType.DMA((tiles // chunk + 3,)),
        ],
        cost=pl.CostEstimate(flops=0, bytes_accessed=6 * tile_data.size, transcendentals=0),
    )

    flops = 2 * tiles * count * size * size
    cost = pl.CostEstimate(flops=flops, bytes_accessed=2 * tile_data.size, transcendentals=0)

    def apply(parts, slots):
        half = shape(F32, members, blk)
        keep_up, send_up, low = call(
            functools.partial(mirror_kernel, slots, evens),
            "mirror",
            [half, half, shape(F32, span)],
            [SMEM] * 2 + [VMEM] * (1 + len(parts)),
            [tile_live, index, tile_data, *parts],
            scratch=[
                pltpu.VMEM((span, count, size), BF16),
                pltpu.VMEM((2 * span + 1, count, size), F32),
            ],
            cost=cost,
        )
        got_up = row_swap(send_up, 1)
        keep_low, send_low = call(
            functools.partial(direct_kernel, slots, evens),
            "direct",
            [half, half],
            [SMEM] * 2 + [VMEM] * (2 + len(parts)),
            [tile_live, index, flipped, low, *parts],
            scratch=[
                pltpu.VMEM((2 * span, count, size), BF16),
                pltpu.VMEM((span + 1, count, size), F32),
            ],
            cost=cost,
        )
        return (keep_up, got_up), (keep_low, row_swap(send_low, 1))

    (pair,) = call(select_kernel, "select", [shape(BF16, 2, blk)], [VMEM] * 3, [vectors, *sent])
    gathered = [pair] + [row_swap(pair, s) for s in range(1, rows)]
    up, low = apply(gathered, [[s] for s in range(rows)])

    code = shape(jnp.int16, members * blk + 1)

    def pair_sum(ours):
        paired, coded = call(
            add_kernel, "add", [shape(F32, members, blk), code], [VMEM] * 2, ours
        )
        return [paired] + [row_swap(coded, g) for g in evens[1:]]

    up = pair_sum(up)
    low = pair_sum(low)
    even, odd, total = call(
        functools.partial(gather_kernel, evens),
        "gather",
        [code] * 2 + [shape(F32, 2, members, blk)],
        [VMEM] * (2 * members),
        low + up,
    )
    (first,) = call(
        functools.partial(first_kernel, evens),
        "first",
        [shape(BF16, 2, members, blk)],
        [SMEM] * 2 + [VMEM] * (3 + members),
        [damp_center, damp_radius, total, pair_swap(odd, 1), pair_swap(even, 0)]
        + [gathered[s] for s in evens],
    )
    up, low = apply([first, row_swap(first, 1)], [evens, [s ^ 1 for s in evens]])

    def pieces(ours):
        parts = call(spread_kernel, "spread", [shape(F32, blk)] * members, [VMEM] * 2, ours)
        return parts[:1] + [row_swap(p, g) for p, g in zip(parts[1:], evens[1:])]

    up = pieces(up)
    low = pieces(low)
    (up,) = call(owner_kernel, "owner", [shape(F32, blk)], [VMEM] * members, up)
    second, first = call(
        second_kernel,
        "second",
        [jax.ShapeDtypeStruct((count, width), F32), jax.ShapeDtypeStruct((count, width), BF16)],
        [SMEM] * 2 + [VMEM] * (4 + members),
        [damp_center, damp_radius, pair, first, pair_swap(up, 0), pair_swap(up, 1), *low],
    )
    return first, second


def solution(mesh):
    placed = (
        P(None, ("col", "row")),
        P(("col", "row"), None, None),
        P(("col", "row")),
        P(("col", "row")),
        P(("col", "row")),
        P(),
        P(),
    )
    return jax.shard_map(
        local,
        mesh=mesh,
        in_specs=placed,
        out_specs=(P(None, ("col", "row")), P(None, ("col", "row"))),
        check_vma=False,
    )
```

```python
import functools

import jax
import jax.numpy as jnp
from jax import lax
from jax.experimental import pallas as pl
from jax.experimental.pallas import tpu as pltpu
from jax.sharding import PartitionSpec as P

VMEM = pl.BlockSpec(memory_space=pltpu.VMEM)
SMEM = pl.BlockSpec(memory_space=pltpu.SMEM)
HBM = pl.BlockSpec(memory_space=pltpu.HBM)
AXES = ("row", "col")
F32, BF16 = jnp.float32, jnp.bfloat16


def call(kernel, name, outs, places, args, scratch=(), cost=None):
    spaces = {id(VMEM): pltpu.VMEM, id(HBM): pltpu.HBM}
    args = [
        pltpu.with_memory_space_constraint(a, spaces[id(p)]) if id(p) in spaces else a
        for a, p in zip(args, places)
    ]
    results = pl.pallas_call(
        kernel,
        out_shape=list(outs),
        in_specs=list(places),
        out_specs=[SMEM if getattr(o, "memory_space", None) == pltpu.SMEM else VMEM for o in outs],
        scratch_shapes=list(scratch),
        compiler_params=pltpu.CompilerParams(vmem_limit_bytes=12 * 1024 * 1024),
        cost_estimate=cost,
        name=name,
    )(*args)
    return list(results)


def row_swap(block, distance):
    rows, cols = lax.axis_size("row"), lax.axis_size("col")
    route = [(r * cols + c, (r ^ distance) * cols + c) for r in range(rows) for c in range(cols)]
    return lax.ppermute(block, AXES, route)


def pair_swap(block, odd):
    rows, cols = lax.axis_size("row"), lax.axis_size("col")
    route = []
    for r in range(rows):
        for c in range(cols):
            other = c + 1 if c % 2 == odd else c - 1
            other = other if 0 <= other < cols else c
            route.append((r * cols + c, (r ^ 1) * cols + other))
    return lax.ppermute(block, AXES, route)


def by_parity(even_case, odd_case):
    parity = lax.rem(lax.axis_index("col"), 2)
    pl.when(parity == 0)(even_case)
    pl.when(parity == 1)(odd_case)


def encode(blocks, out_ref):
    most = jnp.abs(blocks[0])
    for block in blocks[1:]:
        most = jnp.maximum(most, jnp.abs(block))
    most = jnp.broadcast_to(jnp.max(most, axis=1, keepdims=True), most.shape)
    exponent = jnp.ceil(jnp.log2(jnp.maximum(most, 1e-30)))
    scale = jnp.exp2(-exponent) * 32767.0
    for n, block in enumerate(blocks):
        code = jnp.clip(jnp.round(block * scale), -32767.0, 32767.0)
        out_ref[n] = code.astype(jnp.int32).astype(jnp.int16)
    out_ref[len(blocks)] = exponent.astype(jnp.int32).astype(jnp.int16)


def step_of(code_ref):
    exponent = code_ref[code_ref.shape[0] - 1].astype(jnp.int32).astype(F32)
    return jnp.exp2(exponent) * (1.0 / 32767.0)


def decode(code_ref, n, step):
    return code_ref[n].astype(jnp.int32).astype(F32) * step


def load_kernel(chunk, span, blk, row_hbm, offset_hbm, vectors_hbm, tile_hbm, *refs):
    kept_ref, out_ref, flipped_ref, index_ref, row_ref, offset_ref, sems = refs
    count = tile_hbm.shape[0] // chunk
    small = [
        pltpu.make_async_copy(source, target, sems.at[count + n])
        for n, (source, target) in enumerate(
            [
                (row_hbm, row_ref),
                (offset_hbm, offset_ref),
                (vectors_hbm, kept_ref),
            ]
        )
    ]

    def copy(g):
        part = pl.ds(g * chunk, chunk)
        return pltpu.make_async_copy(tile_hbm.at[part], out_ref.at[part], sems.at[g])

    for one in small:
        one.start()
    for g in range(count):
        copy(g).start()
    for one in small:
        one.wait()
    me = lax.axis_index("row")
    for k in range(tile_hbm.shape[0]):
        i = row_ref[0, k]
        j = i + offset_ref[0, k]
        index_ref[0, k] = i ^ (me * blk)
        index_ref[1, k] = jnp.where(j < span, j ^ (me * blk), span + ((j - span) ^ ((me ^ 1) * blk)))
    for g in range(count):
        copy(g).wait()
        for k in range(g * chunk, (g + 1) * chunk):
            flipped_ref[k] = out_ref[k].T


def stack_kernel(*refs):
    parts, out_ref = refs[:-1], refs[-1]
    size = out_ref.shape[-1]
    for s, part in enumerate(parts):
        for b in range(out_ref.shape[1]):
            out_ref[s, b] = part[:, b * size : (b + 1) * size]


def fill(window, half, parts, slots):
    for part, wanted in zip(parts, slots):
        for n, s in enumerate(wanted):
            blk = part.shape[-3]
            for b in range(blk):
                value = part[half, n, b] if len(part.shape) == 5 else part[n, b]
                window[s * blk + b] = value


def split(total, first, evens, keep_ref, send_ref):
    blk = keep_ref.shape[1]
    for n, s in enumerate(evens):
        for b in range(blk):
            keep_ref[n, b] = total[first + s * blk + b]
            send_ref[n, b] = total[first + (s ^ 1) * blk + b]


def mirror_kernel(slots, evens, live_ref, index_ref, tile_ref, *refs):
    parts = refs[: len(slots)]
    keep_ref, send_ref, low_ref, window, total = refs[len(slots) :]
    span = window.shape[0]
    fill(window, 0, parts, slots)
    total[...] = jnp.zeros_like(total)
    for k in range(tile_ref.shape[0]):
        mirrored = jnp.dot(window[index_ref[0, k]], tile_ref[k], preferred_element_type=F32)
        total[jnp.where(k < live_ref[0], index_ref[1, k], 2 * span)] += mirrored
    split(total, span, evens, keep_ref, send_ref)
    low_ref[...] = total[0:span]


def direct_kernel(slots, evens, live_ref, index_ref, flipped_ref, low_ref, *refs):
    parts = refs[:-4]
    keep_ref, send_ref, window, total = refs[-4:]
    span = low_ref.shape[0]
    fill(window, 0, parts[: len(slots)], slots)
    beyond = window.at[span : 2 * span]
    if len(parts) == len(slots):
        fill(beyond, 1, parts, slots)
    else:
        even_ref, odd_ref = parts[len(slots) :]
        inside = lax.axis_index("col") < lax.axis_size("col") - 1

        def odd_case():
            fill(beyond, 1, [odd_ref], slots)

            @pl.when(jnp.logical_not(inside))
            def _():
                beyond[...] = jnp.zeros_like(beyond)

        by_parity(lambda: fill(beyond, 1, [even_ref], slots), odd_case)
    total[0:span] = low_ref[...]
    total[span] = jnp.zeros(total.shape[1:], F32)
    for k in range(flipped_ref.shape[0]):
        direct = jnp.dot(window[index_ref[1, k]], flipped_ref[k], preferred_element_type=F32)
        total[jnp.where(k < live_ref[0], index_ref[0, k], span)] += direct
    split(total, 0, evens, keep_ref, send_ref)


def add_kernel(keep_ref, got_ref, out_ref, code_ref):
    members, blk = out_ref.shape[:2]
    out_ref[...] = keep_ref[...] + got_ref[...]
    encode([out_ref[n, b] for n in range(members) for b in range(blk)], code_ref)


def gather_kernel(evens, *refs):
    members = len(evens)
    halves = refs[:members], refs[members : 2 * members]
    even_ref, odd_ref, sum_ref = refs[2 * members :]
    blk = sum_ref.shape[2]
    place = {s: n for n, s in enumerate(evens)}
    for half, (own_ref, *others) in enumerate(halves):
        steps = [step_of(other) for other in others]
        for n, s in enumerate(evens):
            for b in range(blk):
                value = own_ref[n, b]
                for other, step, g in zip(others, steps, evens[1:]):
                    value = value + decode(other, place[s ^ g] * blk + b, step)
                sum_ref[half, n, b] = value

    def code(half, out_ref):
        encode([sum_ref[half, n, b] for n in range(members) for b in range(blk)], out_ref)

    def even_case():
        code(1, even_ref)
        code(0, odd_ref)

    def odd_case():
        code(0, even_ref)
        code(1, odd_ref)

    by_parity(even_case, odd_case)


def first_kernel(evens, center_ref, radius_ref, own_ref, own_even_ref, own_odd_ref, sum_ref, odd_ref, even_ref, out_ref):
    col = lax.axis_index("col")
    center, radius = center_ref[0], radius_ref[0]

    def degree(image, vectors):
        return ((image - center * vectors.astype(F32)) / radius).astype(BF16)

    def both(from_previous, from_next, next_ref):
        inside = col < lax.axis_size("col") - 1
        blk = out_ref.shape[2]
        previous_step, next_step = step_of(from_previous), step_of(from_next)
        for n, s in enumerate(evens):
            for b in range(blk):
                arrived = decode(from_previous, n * blk + b, previous_step)
                arrived = jnp.where(col > 0, arrived, 0.0)
                out_ref[0, n, b] = degree(sum_ref[0, n, b] + arrived, own_ref[s, b])
                arrived = decode(from_next, n * blk + b, next_step)
                beyond = degree(sum_ref[1, n, b] + arrived, next_ref[s, b])
                out_ref[1, n, b] = jnp.where(inside, beyond, jnp.zeros_like(beyond))

    by_parity(
        lambda: both(odd_ref, even_ref, own_even_ref), lambda: both(even_ref, odd_ref, own_odd_ref)
    )


def spread_kernel(keep_ref, got_ref, *outs):
    for n, out_ref in enumerate(outs):
        out_ref[...] = keep_ref[n] + got_ref[n]


def owner_kernel(*refs):
    parts, out_ref = refs[:-1], refs[-1]
    total = parts[0][...]
    for part in parts[1:]:
        total = total + part[...]
    out_ref[...] = total


def second_kernel(center_ref, radius_ref, own_ref, first_ref, even_ref, odd_ref, *refs):
    parts, (out_ref, first_out_ref) = refs[:-2], refs[-2:]
    col = lax.axis_index("col")
    center, radius = center_ref[0], radius_ref[0]
    blk, _, size = even_ref.shape

    def finish(from_previous):
        for b in range(blk):
            image = jnp.where(col > 0, from_previous[b], 0.0)
            for part in parts:
                image = image + part[b]
            first = first_ref[0, 0, b].astype(F32)
            second = 2.0 * (image - center * first) / radius - own_ref[0, b].astype(F32)
            out_ref[:, b * size : (b + 1) * size] = second

    for b in range(blk):
        first_out_ref[:, b * size : (b + 1) * size] = first_ref[0, 0, b]
    by_parity(lambda: finish(odd_ref), lambda: finish(even_ref))


def local(vectors, tile_data, tile_row, tile_offset, tile_live, damp_center, damp_radius):
    rows = lax.axis_size("row")
    count, width = vectors.shape
    tiles, size, _ = tile_data.shape
    blk = width // size
    span = rows * blk
    evens = [s for s in range(rows) if bin(s).count("1") % 2 == 0]
    members = len(evens)

    def shape(dtype, *lead):
        return pltpu.VMEM((*lead, count, size), dtype)

    sent = [row_swap(vectors, s) for s in range(1, rows)]
    kept = pltpu.VMEM(tile_data.shape, BF16)
    chunk = 8
    vectors, tile_data, flipped, index = call(
        functools.partial(load_kernel, chunk, span, blk),
        "load",
        [pltpu.VMEM(vectors.shape, BF16), kept, kept, pltpu.SMEM((2, tiles), jnp.int32)],
        [HBM] * 4,
        [tile_row.reshape(1, tiles), tile_offset.reshape(1, tiles), vectors, tile_data],
        scratch=[
            pltpu.SMEM((1, tiles), jnp.int32),
            pltpu.SMEM((1, tiles), jnp.int32),
            pltpu.SemaphoreType.DMA((tiles // chunk + 3,)),
        ],
        cost=pl.CostEstimate(flops=0, bytes_accessed=6 * tile_data.size, transcendentals=0),
    )

    flops = 2 * tiles * count * size * size
    cost = pl.CostEstimate(flops=flops, bytes_accessed=2 * tile_data.size, transcendentals=0)

    def apply(parts, slots, arrived=()):
        half = shape(F32, members, blk)
        keep_up, send_up, low = call(
            functools.partial(mirror_kernel, slots, evens),
            "mirror",
            [half, half, shape(F32, span)],
            [SMEM] * 2 + [VMEM] * (1 + len(parts)),
            [tile_live, index, tile_data, *parts],
            scratch=[
                pltpu.VMEM((span, count, size), BF16),
                pltpu.VMEM((2 * span + 1, count, size), F32),
            ],
            cost=cost,
        )
        got_up = row_swap(send_up, 1)
        keep_low, send_low = call(
            functools.partial(direct_kernel, slots, evens),
            "direct",
            [half, half],
            [SMEM] * 2 + [VMEM] * (2 + len(parts) + len(arrived)),
            [tile_live, index, flipped, low, *parts, *arrived],
            scratch=[
                pltpu.VMEM((2 * span, count, size), BF16),
                pltpu.VMEM((span + 1, count, size), F32),
            ],
            cost=cost,
        )
        return (keep_up, got_up), (keep_low, row_swap(send_low, 1))

    (own,) = call(
        stack_kernel, "stack", [shape(BF16, rows, blk)], [VMEM] * rows, [vectors, *sent]
    )
    arrived = [pair_swap(own, 0), pair_swap(own, 1)]
    up, low = apply([own], [list(range(rows))], arrived)
    code = shape(jnp.int16, members * blk + 1)

    def pair_sum(ours):
        paired, coded = call(
            add_kernel, "add", [shape(F32, members, blk), code], [VMEM] * 2, ours
        )
        return [paired] + [row_swap(coded, g) for g in evens[1:]]

    up = pair_sum(up)
    low = pair_sum(low)
    even, odd, total = call(
        functools.partial(gather_kernel, evens),
        "gather",
        [code] * 2 + [shape(F32, 2, members, blk)],
        [VMEM] * (2 * members),
        low + up,
    )
    (first,) = call(
        functools.partial(first_kernel, evens),
        "first",
        [shape(BF16, 2, members, blk)],
        [SMEM] * 2 + [VMEM] * 6,
        [damp_center, damp_radius, own, *arrived, total, pair_swap(odd, 1), pair_swap(even, 0)],
    )
    up, low = apply([first, row_swap(first, 1)], [evens, [s ^ 1 for s in evens]])

    def pieces(ours):
        parts = call(spread_kernel, "spread", [shape(F32, blk)] * members, [VMEM] * 2, ours)
        return parts[:1] + [row_swap(p, g) for p, g in zip(parts[1:], evens[1:])]

    up = pieces(up)
    low = pieces(low)
    (up,) = call(owner_kernel, "owner", [shape(F32, blk)], [VMEM] * members, up)
    second, first = call(
        second_kernel,
        "second",
        [jax.ShapeDtypeStruct((count, width), F32), jax.ShapeDtypeStruct((count, width), BF16)],
        [SMEM] * 2 + [VMEM] * (4 + members),
        [damp_center, damp_radius, own, first, pair_swap(up, 0), pair_swap(up, 1), *low],
    )
    return first, second


def solution(mesh):
    placed = (
        P(None, ("col", "row")),
        P(("col", "row"), None, None),
        P(("col", "row")),
        P(("col", "row")),
        P(("col", "row")),
        P(),
        P(),
    )
    return jax.shard_map(
        local,
        mesh=mesh,
        in_specs=placed,
        out_specs=(P(None, ("col", "row")), P(None, ("col", "row"))),
        check_vma=False,
    )
```

```python
import functools

import jax
import jax.numpy as jnp
from jax import lax
from jax.experimental import pallas as pl
from jax.experimental.pallas import tpu as pltpu
from jax.sharding import PartitionSpec as P

VMEM = pl.BlockSpec(memory_space=pltpu.VMEM)
SMEM = pl.BlockSpec(memory_space=pltpu.SMEM)
HBM = pl.BlockSpec(memory_space=pltpu.HBM)
AXES = ("row", "col")
F32, BF16 = jnp.float32, jnp.bfloat16


def call(kernel, name, outs, places, args, scratch=(), cost=None):
    spaces = {id(VMEM): pltpu.VMEM, id(HBM): pltpu.HBM}
    args = [
        pltpu.with_memory_space_constraint(a, spaces[id(p)]) if id(p) in spaces else a
        for a, p in zip(args, places)
    ]
    results = pl.pallas_call(
        kernel,
        out_shape=list(outs),
        in_specs=list(places),
        out_specs=[SMEM if getattr(o, "memory_space", None) == pltpu.SMEM else VMEM for o in outs],
        scratch_shapes=list(scratch),
        compiler_params=pltpu.CompilerParams(vmem_limit_bytes=12 * 1024 * 1024),
        cost_estimate=cost,
        name=name,
    )(*args)
    return list(results)


def row_swap(block, distance):
    rows, cols = lax.axis_size("row"), lax.axis_size("col")
    route = [(r * cols + c, (r ^ distance) * cols + c) for r in range(rows) for c in range(cols)]
    return lax.ppermute(block, AXES, route)


def pair_swap(block, odd):
    rows, cols = lax.axis_size("row"), lax.axis_size("col")
    route = []
    for r in range(rows):
        for c in range(cols):
            other = c + 1 if c % 2 == odd else c - 1
            other = other if 0 <= other < cols else c
            route.append((r * cols + c, (r ^ 1) * cols + other))
    return lax.ppermute(block, AXES, route)


def by_parity(even_case, odd_case):
    parity = lax.rem(lax.axis_index("col"), 2)
    pl.when(parity == 0)(even_case)
    pl.when(parity == 1)(odd_case)


def encode(blocks, out_ref):
    most = jnp.abs(blocks[0])
    for block in blocks[1:]:
        most = jnp.maximum(most, jnp.abs(block))
    most = jnp.broadcast_to(jnp.max(most, axis=1, keepdims=True), most.shape)
    exponent = jnp.ceil(jnp.log2(jnp.maximum(most, 1e-30)))
    scale = jnp.exp2(-exponent) * 32767.0
    for n, block in enumerate(blocks):
        code = jnp.clip(jnp.round(block * scale), -32767.0, 32767.0)
        out_ref[n] = code.astype(jnp.int32).astype(jnp.int16)
    out_ref[len(blocks)] = exponent.astype(jnp.int32).astype(jnp.int16)


def step_of(code_ref):
    exponent = code_ref[code_ref.shape[0] - 1].astype(jnp.int32).astype(F32)
    return jnp.exp2(exponent) * (1.0 / 32767.0)


def decode(code_ref, n, step):
    return code_ref[n].astype(jnp.int32).astype(F32) * step


def load_kernel(chunk, span, blk, row_hbm, offset_hbm, vectors_hbm, tile_hbm, *refs):
    kept_ref, out_ref, flipped_ref, index_ref, row_ref, offset_ref, sems = refs
    count = tile_hbm.shape[0] // chunk
    size = tile_hbm.shape[-1]
    small = [
        pltpu.make_async_copy(source, target, sems.at[2 * count + n])
        for n, (source, target) in enumerate(
            [
                (row_hbm, row_ref),
                (offset_hbm, offset_ref),
                (vectors_hbm, kept_ref),
            ]
        )
    ]

    def copies(g):
        part = pl.ds(g * chunk, chunk)
        return [
            pltpu.make_async_copy(
                tile_hbm.at[part, side],
                out_ref.at[part, :, side * size : (side + 1) * size],
                sems.at[2 * g + side],
            )
            for side in range(2)
        ]

    for one in small:
        one.start()
    for g in range(count):
        for one in copies(g):
            one.start()
    for one in small:
        one.wait()
    me = lax.axis_index("row")
    for k in range(row_ref.shape[1]):
        i = row_ref[0, k]
        j = i + offset_ref[0, k]
        index_ref[0, k] = i ^ (me * blk)
        index_ref[1, k] = jnp.where(j < span, j ^ (me * blk), span + ((j - span) ^ ((me ^ 1) * blk)))
    for g in range(count):
        for one in copies(g):
            one.wait()
        for p in range(g * chunk, (g + 1) * chunk):
            for side in range(2):
                place = slice(side * size, (side + 1) * size)
                flipped_ref[p, :, place] = out_ref[p, :, place].T


def stack_kernel(*refs):
    parts, out_ref = refs[:-1], refs[-1]
    size = out_ref.shape[-1]
    for s, part in enumerate(parts):
        for b in range(out_ref.shape[1]):
            out_ref[s, b] = part[:, b * size : (b + 1) * size]


def fill(window, half, parts, slots):
    for part, wanted in zip(parts, slots):
        for n, s in enumerate(wanted):
            blk = part.shape[-3]
            for b in range(blk):
                value = part[half, n, b] if len(part.shape) == 5 else part[n, b]
                window[s * blk + b] = value


def split(total, other, first, evens, keep_ref, send_ref):
    blk = keep_ref.shape[1]
    for n, s in enumerate(evens):
        for b in range(blk):
            kept, sent = first + s * blk + b, first + (s ^ 1) * blk + b
            keep_ref[n, b] = total[kept] + other[kept]
            send_ref[n, b] = total[sent] + other[sent]


def products(pairs_ref, window, index_ref, source, target, live_ref, *totals):
    spare = totals[0].shape[0] - 1
    for p in range(pairs_ref.shape[0]):
        stacked = jnp.concatenate([window[index_ref[source, 2 * p + side]] for side in range(2)], axis=0)
        result = jnp.dot(stacked, pairs_ref[p], preferred_element_type=F32)
        count, size = result.shape[0] // 2, result.shape[1] // 2
        for side in range(2):
            k = 2 * p + side
            to = jnp.where(k < live_ref[0], index_ref[target, k], spare)
            totals[side][to] += result[side * count : (side + 1) * count, side * size : (side + 1) * size]


def mirror_kernel(slots, evens, live_ref, index_ref, tile_ref, *refs):
    parts = refs[: len(slots)]
    keep_ref, send_ref, low_ref, window, total, other = refs[len(slots) :]
    span = window.shape[0]
    fill(window, 0, parts, slots)
    total[...] = jnp.zeros_like(total)
    other[...] = jnp.zeros_like(other)
    products(tile_ref, window, index_ref, 0, 1, live_ref, total, other)
    split(total, other, span, evens, keep_ref, send_ref)
    low_ref[...] = total[0:span] + other[0:span]


def direct_kernel(slots, evens, live_ref, index_ref, flipped_ref, low_ref, *refs):
    parts = refs[:-5]
    keep_ref, send_ref, window, total, other = refs[-5:]
    span = low_ref.shape[0]
    fill(window, 0, parts[: len(slots)], slots)
    beyond = window.at[span : 2 * span]
    if len(parts) == len(slots):
        fill(beyond, 1, parts, slots)
    else:
        even_ref, odd_ref = parts[len(slots) :]
        inside = lax.axis_index("col") < lax.axis_size("col") - 1

        def odd_case():
            fill(beyond, 1, [odd_ref], slots)

            @pl.when(jnp.logical_not(inside))
            def _():
                beyond[...] = jnp.zeros_like(beyond)

        by_parity(lambda: fill(beyond, 1, [even_ref], slots), odd_case)
    total[0:span] = low_ref[...]
    total[span] = jnp.zeros(total.shape[1:], F32)
    other[...] = jnp.zeros_like(other)
    products(flipped_ref, window, index_ref, 1, 0, live_ref, total, other)
    split(total, other, 0, evens, keep_ref, send_ref)


def add_kernel(keep_ref, got_ref, out_ref, code_ref):
    members, blk = out_ref.shape[:2]
    out_ref[...] = keep_ref[...] + got_ref[...]
    encode([out_ref[n, b] for n in range(members) for b in range(blk)], code_ref)


def gather_kernel(evens, *refs):
    members = len(evens)
    halves = refs[:members], refs[members : 2 * members]
    even_ref, odd_ref, sum_ref = refs[2 * members :]
    blk = sum_ref.shape[2]
    place = {s: n for n, s in enumerate(evens)}
    for half, (own_ref, *others) in enumerate(halves):
        steps = [step_of(other) for other in others]
        for n, s in enumerate(evens):
            for b in range(blk):
                value = own_ref[n, b]
                for other, step, g in zip(others, steps, evens[1:]):
                    value = value + decode(other, place[s ^ g] * blk + b, step)
                sum_ref[half, n, b] = value

    def code(half, out_ref):
        encode([sum_ref[half, n, b] for n in range(members) for b in range(blk)], out_ref)

    def even_case():
        code(1, even_ref)
        code(0, odd_ref)

    def odd_case():
        code(0, even_ref)
        code(1, odd_ref)

    by_parity(even_case, odd_case)


def first_kernel(evens, center_ref, radius_ref, own_ref, own_even_ref, own_odd_ref, sum_ref, odd_ref, even_ref, out_ref):
    col = lax.axis_index("col")
    center, radius = center_ref[0], radius_ref[0]

    def degree(image, vectors):
        return ((image - center * vectors.astype(F32)) / radius).astype(BF16)

    def both(from_previous, from_next, next_ref):
        inside = col < lax.axis_size("col") - 1
        blk = out_ref.shape[2]
        previous_step, next_step = step_of(from_previous), step_of(from_next)
        for n, s in enumerate(evens):
            for b in range(blk):
                arrived = decode(from_previous, n * blk + b, previous_step)
                arrived = jnp.where(col > 0, arrived, 0.0)
                out_ref[0, n, b] = degree(sum_ref[0, n, b] + arrived, own_ref[s, b])
                arrived = decode(from_next, n * blk + b, next_step)
                beyond = degree(sum_ref[1, n, b] + arrived, next_ref[s, b])
                out_ref[1, n, b] = jnp.where(inside, beyond, jnp.zeros_like(beyond))

    by_parity(
        lambda: both(odd_ref, even_ref, own_even_ref), lambda: both(even_ref, odd_ref, own_odd_ref)
    )


def spread_kernel(keep_ref, got_ref, *outs):
    for n, out_ref in enumerate(outs):
        out_ref[...] = keep_ref[n] + got_ref[n]


def owner_kernel(*refs):
    parts, out_ref = refs[:-1], refs[-1]
    total = parts[0][...]
    for part in parts[1:]:
        total = total + part[...]
    out_ref[...] = total


def second_kernel(center_ref, radius_ref, own_ref, first_ref, even_ref, odd_ref, *refs):
    parts, (out_ref, first_out_ref) = refs[:-2], refs[-2:]
    col = lax.axis_index("col")
    center, radius = center_ref[0], radius_ref[0]
    blk, _, size = even_ref.shape

    def finish(from_previous):
        for b in range(blk):
            image = jnp.where(col > 0, from_previous[b], 0.0)
            for part in parts:
                image = image + part[b]
            first = first_ref[0, 0, b].astype(F32)
            second = 2.0 * (image - center * first) / radius - own_ref[0, b].astype(F32)
            out_ref[:, b * size : (b + 1) * size] = second

    for b in range(blk):
        first_out_ref[:, b * size : (b + 1) * size] = first_ref[0, 0, b]
    by_parity(lambda: finish(odd_ref), lambda: finish(even_ref))


def local(vectors, tile_data, tile_row, tile_offset, tile_live, damp_center, damp_radius):
    rows = lax.axis_size("row")
    count, width = vectors.shape
    tiles, size, _ = tile_data.shape
    blk = width // size
    span = rows * blk
    evens = [s for s in range(rows) if bin(s).count("1") % 2 == 0]
    members = len(evens)

    def shape(dtype, *lead):
        return pltpu.VMEM((*lead, count, size), dtype)

    sent = [row_swap(vectors, s) for s in range(1, rows)]
    kept = pltpu.VMEM((tiles // 2, size, 2 * size), BF16)
    chunk = 4
    vectors, tile_data, flipped, index = call(
        functools.partial(load_kernel, chunk, span, blk),
        "load",
        [pltpu.VMEM(vectors.shape, BF16), kept, kept, pltpu.SMEM((2, tiles), jnp.int32)],
        [HBM] * 4,
        [tile_row.reshape(1, tiles), tile_offset.reshape(1, tiles), vectors]
        + [tile_data.reshape(tiles // 2, 2, size, size)],
        scratch=[
            pltpu.SMEM((1, tiles), jnp.int32),
            pltpu.SMEM((1, tiles), jnp.int32),
            pltpu.SemaphoreType.DMA((tiles // chunk + 3,)),
        ],
        cost=pl.CostEstimate(flops=0, bytes_accessed=6 * tile_data.size, transcendentals=0),
    )

    flops = 2 * tiles * count * size * size
    cost = pl.CostEstimate(flops=flops, bytes_accessed=2 * tile_data.size, transcendentals=0)

    def apply(parts, slots, arrived=()):
        half = shape(F32, members, blk)
        keep_up, send_up, low = call(
            functools.partial(mirror_kernel, slots, evens),
            "mirror",
            [half, half, shape(F32, span)],
            [SMEM] * 2 + [VMEM] * (1 + len(parts)),
            [tile_live, index, tile_data, *parts],
            scratch=[
                pltpu.VMEM((span, count, size), BF16),
                pltpu.VMEM((2 * span + 1, count, size), F32),
                pltpu.VMEM((2 * span + 1, count, size), F32),
            ],
            cost=cost,
        )
        got_up = row_swap(send_up, 1)
        keep_low, send_low = call(
            functools.partial(direct_kernel, slots, evens),
            "direct",
            [half, half],
            [SMEM] * 2 + [VMEM] * (2 + len(parts) + len(arrived)),
            [tile_live, index, flipped, low, *parts, *arrived],
            scratch=[
                pltpu.VMEM((2 * span, count, size), BF16),
                pltpu.VMEM((span + 1, count, size), F32),
                pltpu.VMEM((span + 1, count, size), F32),
            ],
            cost=cost,
        )
        return (keep_up, got_up), (keep_low, row_swap(send_low, 1))

    (own,) = call(
        stack_kernel, "stack", [shape(BF16, rows, blk)], [VMEM] * rows, [vectors, *sent]
    )
    arrived = [pair_swap(own, 0), pair_swap(own, 1)]
    up, low = apply([own], [list(range(rows))], arrived)
    code = shape(jnp.int16, members * blk + 1)

    def pair_sum(ours):
        paired, coded = call(
            add_kernel, "add", [shape(F32, members, blk), code], [VMEM] * 2, ours
        )
        return [paired] + [row_swap(coded, g) for g in evens[1:]]

    up = pair_sum(up)
    low = pair_sum(low)
    even, odd, total = call(
        functools.partial(gather_kernel, evens),
        "gather",
        [code] * 2 + [shape(F32, 2, members, blk)],
        [VMEM] * (2 * members),
        low + up,
    )
    (first,) = call(
        functools.partial(first_kernel, evens),
        "first",
        [shape(BF16, 2, members, blk)],
        [SMEM] * 2 + [VMEM] * 6,
        [damp_center, damp_radius, own, *arrived, total, pair_swap(odd, 1), pair_swap(even, 0)],
    )
    up, low = apply([first, row_swap(first, 1)], [evens, [s ^ 1 for s in evens]])

    def pieces(ours):
        parts = call(spread_kernel, "spread", [shape(F32, blk)] * members, [VMEM] * 2, ours)
        return parts[:1] + [row_swap(p, g) for p, g in zip(parts[1:], evens[1:])]

    up = pieces(up)
    low = pieces(low)
    (up,) = call(owner_kernel, "owner", [shape(F32, blk)], [VMEM] * members, up)
    second, first = call(
        second_kernel,
        "second",
        [jax.ShapeDtypeStruct((count, width), F32), jax.ShapeDtypeStruct((count, width), BF16)],
        [SMEM] * 2 + [VMEM] * (4 + members),
        [damp_center, damp_radius, own, first, pair_swap(up, 0), pair_swap(up, 1), *low],
    )
    return first, second


def solution(mesh):
    placed = (
        P(None, ("col", "row")),
        P(("col", "row"), None, None),
        P(("col", "row")),
        P(("col", "row")),
        P(("col", "row")),
        P(),
        P(),
    )
    return jax.shard_map(
        local,
        mesh=mesh,
        in_specs=placed,
        out_specs=(P(None, ("col", "row")), P(None, ("col", "row"))),
        check_vma=False,
    )
```

```python
import functools

import jax
import jax.numpy as jnp
from jax import lax
from jax.experimental import pallas as pl
from jax.experimental.pallas import tpu as pltpu
from jax.sharding import PartitionSpec as P

VMEM = pl.BlockSpec(memory_space=pltpu.VMEM)
SMEM = pl.BlockSpec(memory_space=pltpu.SMEM)
HBM = pl.BlockSpec(memory_space=pltpu.HBM)
AXES = ("row", "col")
F32, BF16 = jnp.float32, jnp.bfloat16


def call(kernel, name, outs, places, args, scratch=(), cost=None):
    spaces = {id(VMEM): pltpu.VMEM, id(HBM): pltpu.HBM}
    args = [
        pltpu.with_memory_space_constraint(a, spaces[id(p)]) if id(p) in spaces else a
        for a, p in zip(args, places)
    ]
    results = pl.pallas_call(
        kernel,
        out_shape=list(outs),
        in_specs=list(places),
        out_specs=[SMEM if getattr(o, "memory_space", None) == pltpu.SMEM else VMEM for o in outs],
        scratch_shapes=list(scratch),
        compiler_params=pltpu.CompilerParams(vmem_limit_bytes=12 * 1024 * 1024),
        cost_estimate=cost,
        name=name,
    )(*args)
    return list(results)


def row_swap(block, distance):
    rows, cols = lax.axis_size("row"), lax.axis_size("col")
    route = [(r * cols + c, (r ^ distance) * cols + c) for r in range(rows) for c in range(cols)]
    return lax.ppermute(block, AXES, route)


def pair_swap(block, odd):
    rows, cols = lax.axis_size("row"), lax.axis_size("col")
    route = []
    for r in range(rows):
        for c in range(cols):
            other = c + 1 if c % 2 == odd else c - 1
            other = other if 0 <= other < cols else c
            route.append((r * cols + c, (r ^ 1) * cols + other))
    return lax.ppermute(block, AXES, route)


def by_parity(even_case, odd_case):
    parity = lax.rem(lax.axis_index("col"), 2)
    pl.when(parity == 0)(even_case)
    pl.when(parity == 1)(odd_case)


ROWS = 16


def encode(blocks, out_ref):
    parts = [block[r : r + ROWS] for block in blocks for r in range(0, block.shape[0], ROWS)]
    most = jnp.abs(parts[0])
    for part in parts[1:]:
        most = jnp.maximum(most, jnp.abs(part))
    exponent = jnp.ceil(jnp.log2(jnp.maximum(most, 1e-30)))
    scale = jnp.exp2(-exponent) * 32767.0
    for n, part in enumerate(parts):
        code = jnp.clip(jnp.round(part * scale), -32767.0, 32767.0)
        out_ref[n * ROWS : (n + 1) * ROWS] = code.astype(jnp.int32).astype(jnp.int16)
    out_ref[len(parts) * ROWS :] = exponent.astype(jnp.int32).astype(jnp.int16)


def step_of(code_ref, height):
    exponent = code_ref[code_ref.shape[0] - ROWS :].astype(jnp.int32).astype(F32)
    return jnp.concatenate([jnp.exp2(exponent) * (1.0 / 32767.0)] * (height // ROWS), axis=0)


def decode(code_ref, n, step):
    height = step.shape[0]
    return code_ref[n * height : (n + 1) * height].astype(jnp.int32).astype(F32) * step


def load_kernel(chunk, span, blk, row_hbm, offset_hbm, vectors_hbm, tile_hbm, *refs):
    kept_ref, out_ref, flipped_ref, index_ref, row_ref, offset_ref, sems = refs
    count = tile_hbm.shape[0] // chunk
    size = tile_hbm.shape[-1]
    small = [
        pltpu.make_async_copy(source, target, sems.at[2 * count + n])
        for n, (source, target) in enumerate(
            [
                (row_hbm, row_ref),
                (offset_hbm, offset_ref),
                (vectors_hbm, kept_ref),
            ]
        )
    ]

    def copies(g):
        part = pl.ds(g * chunk, chunk)
        return [
            pltpu.make_async_copy(
                tile_hbm.at[part, side],
                out_ref.at[part, :, side * size : (side + 1) * size],
                sems.at[2 * g + side],
            )
            for side in range(2)
        ]

    for one in small:
        one.start()
    for g in range(count):
        for one in copies(g):
            one.start()
    for one in small:
        one.wait()
    me = lax.axis_index("row")
    for k in range(row_ref.shape[1]):
        i = row_ref[0, k]
        j = i + offset_ref[0, k]
        index_ref[0, k] = i ^ (me * blk)
        index_ref[1, k] = jnp.where(j < span, j ^ (me * blk), span + ((j - span) ^ ((me ^ 1) * blk)))
    for g in range(count):
        for one in copies(g):
            one.wait()
        for p in range(g * chunk, (g + 1) * chunk):
            for side in range(2):
                place = slice(side * size, (side + 1) * size)
                flipped_ref[p, :, place] = out_ref[p, :, place].T


def stack_kernel(*refs):
    parts, out_ref = refs[:-1], refs[-1]
    size = out_ref.shape[-1]
    for s, part in enumerate(parts):
        for b in range(out_ref.shape[1]):
            out_ref[s, b] = part[:, b * size : (b + 1) * size]


def fill(window, half, parts, slots):
    for part, wanted in zip(parts, slots):
        for n, s in enumerate(wanted):
            blk = part.shape[-3]
            for b in range(blk):
                value = part[half, n, b] if len(part.shape) == 5 else part[n, b]
                window[s * blk + b] = value


def split(total, other, first, evens, keep_ref, send_ref):
    blk = keep_ref.shape[1]
    for n, s in enumerate(evens):
        for b in range(blk):
            kept, sent = first + s * blk + b, first + (s ^ 1) * blk + b
            keep_ref[n, b] = total[kept] + other[kept]
            send_ref[n, b] = total[sent] + other[sent]


def products(pairs_ref, window, index_ref, source, target, live_ref, *totals):
    spare = totals[0].shape[0] - 1
    for p in range(pairs_ref.shape[0]):
        stacked = jnp.concatenate([window[index_ref[source, 2 * p + side]] for side in range(2)], axis=0)
        result = jnp.dot(stacked, pairs_ref[p], preferred_element_type=F32)
        count, size = result.shape[0] // 2, result.shape[1] // 2
        for side in range(2):
            k = 2 * p + side
            to = jnp.where(k < live_ref[0], index_ref[target, k], spare)
            totals[side][to] += result[side * count : (side + 1) * count, side * size : (side + 1) * size]


def mirror_kernel(slots, evens, live_ref, index_ref, tile_ref, *refs):
    parts = refs[: len(slots)]
    keep_ref, send_ref, low_ref, window, total, other = refs[len(slots) :]
    span = window.shape[0]
    fill(window, 0, parts, slots)
    total[...] = jnp.zeros_like(total)
    other[...] = jnp.zeros_like(other)
    products(tile_ref, window, index_ref, 0, 1, live_ref, total, other)
    split(total, other, span, evens, keep_ref, send_ref)
    low_ref[...] = total[0:span] + other[0:span]


def direct_kernel(slots, evens, live_ref, index_ref, flipped_ref, low_ref, *refs):
    parts = refs[:-5]
    keep_ref, send_ref, window, total, other = refs[-5:]
    span = low_ref.shape[0]
    fill(window, 0, parts[: len(slots)], slots)
    beyond = window.at[span : 2 * span]
    if len(parts) == len(slots):
        fill(beyond, 1, parts, slots)
    else:
        even_ref, odd_ref = parts[len(slots) :]
        inside = lax.axis_index("col") < lax.axis_size("col") - 1

        def odd_case():
            fill(beyond, 1, [odd_ref], slots)

            @pl.when(jnp.logical_not(inside))
            def _():
                beyond[...] = jnp.zeros_like(beyond)

        by_parity(lambda: fill(beyond, 1, [even_ref], slots), odd_case)
    total[0:span] = low_ref[...]
    total[span] = jnp.zeros(total.shape[1:], F32)
    other[...] = jnp.zeros_like(other)
    products(flipped_ref, window, index_ref, 1, 0, live_ref, total, other)
    split(total, other, 0, evens, keep_ref, send_ref)


def add_kernel(keep_ref, got_ref, out_ref, code_ref):
    members, blk = out_ref.shape[:2]
    out_ref[...] = keep_ref[...] + got_ref[...]
    encode([out_ref[n, b] for n in range(members) for b in range(blk)], code_ref)


def gather_kernel(evens, *refs):
    members = len(evens)
    halves = refs[:members], refs[members : 2 * members]
    even_ref, odd_ref, sum_ref = refs[2 * members :]
    blk = sum_ref.shape[2]
    place = {s: n for n, s in enumerate(evens)}
    for half, (own_ref, *others) in enumerate(halves):
        steps = [step_of(other, own_ref.shape[2]) for other in others]
        for n, s in enumerate(evens):
            for b in range(blk):
                value = own_ref[n, b]
                for other, step, g in zip(others, steps, evens[1:]):
                    value = value + decode(other, place[s ^ g] * blk + b, step)
                sum_ref[half, n, b] = value

    def code(half, out_ref):
        encode([sum_ref[half, n, b] for n in range(members) for b in range(blk)], out_ref)

    def even_case():
        code(1, even_ref)
        code(0, odd_ref)

    def odd_case():
        code(0, even_ref)
        code(1, odd_ref)

    by_parity(even_case, odd_case)


def first_kernel(evens, center_ref, radius_ref, own_ref, own_even_ref, own_odd_ref, sum_ref, odd_ref, even_ref, out_ref):
    col = lax.axis_index("col")
    center, radius = center_ref[0], radius_ref[0]

    def degree(image, vectors):
        return ((image - center * vectors.astype(F32)) / radius).astype(BF16)

    def both(from_previous, from_next, next_ref):
        inside = col < lax.axis_size("col") - 1
        blk = out_ref.shape[2]
        height = out_ref.shape[3]
        previous_step, next_step = step_of(from_previous, height), step_of(from_next, height)
        for n, s in enumerate(evens):
            for b in range(blk):
                arrived = decode(from_previous, n * blk + b, previous_step)
                arrived = jnp.where(col > 0, arrived, 0.0)
                out_ref[0, n, b] = degree(sum_ref[0, n, b] + arrived, own_ref[s, b])
                arrived = decode(from_next, n * blk + b, next_step)
                beyond = degree(sum_ref[1, n, b] + arrived, next_ref[s, b])
                out_ref[1, n, b] = jnp.where(inside, beyond, jnp.zeros_like(beyond))

    by_parity(
        lambda: both(odd_ref, even_ref, own_even_ref), lambda: both(even_ref, odd_ref, own_odd_ref)
    )


def spread_kernel(keep_ref, got_ref, own_ref, *outs):
    own_ref[...] = keep_ref[0] + got_ref[0]
    for n, out_ref in enumerate(outs, 1):
        encode([keep_ref[n, b] + got_ref[n, b] for b in range(keep_ref.shape[1])], out_ref)


def total_of(own_ref, others, b):
    value = own_ref[b]
    for other in others:
        value = value + decode(other, b, step_of(other, own_ref.shape[1]))
    return value


def owner_kernel(own_ref, *refs):
    encode([total_of(own_ref, refs[:-1], b) for b in range(own_ref.shape[0])], refs[-1])


def second_kernel(center_ref, radius_ref, own_ref, first_ref, even_ref, odd_ref, *refs):
    (low_ref, *others), (out_ref, first_out_ref) = refs[:-2], refs[-2:]
    col = lax.axis_index("col")
    center, radius = center_ref[0], radius_ref[0]
    blk, height, size = low_ref.shape

    def finish(from_previous):
        step = step_of(from_previous, height)
        for b in range(blk):
            arrived = jnp.where(col > 0, decode(from_previous, b, step), 0.0)
            image = total_of(low_ref, others, b) + arrived
            first = first_ref[0, 0, b].astype(F32)
            second = 2.0 * (image - center * first) / radius - own_ref[0, b].astype(F32)
            out_ref[:, b * size : (b + 1) * size] = second

    for b in range(blk):
        first_out_ref[:, b * size : (b + 1) * size] = first_ref[0, 0, b]
    by_parity(lambda: finish(odd_ref), lambda: finish(even_ref))


def local(vectors, tile_data, tile_row, tile_offset, tile_live, damp_center, damp_radius):
    rows = lax.axis_size("row")
    count, width = vectors.shape
    tiles, size, _ = tile_data.shape
    blk = width // size
    span = rows * blk
    evens = [s for s in range(rows) if bin(s).count("1") % 2 == 0]
    members = len(evens)

    def shape(dtype, *lead):
        return pltpu.VMEM((*lead, count, size), dtype)

    sent = [row_swap(vectors, s) for s in range(1, rows)]
    kept = pltpu.VMEM((tiles // 2, size, 2 * size), BF16)
    chunk = 4
    vectors, tile_data, flipped, index = call(
        functools.partial(load_kernel, chunk, span, blk),
        "load",
        [pltpu.VMEM(vectors.shape, BF16), kept, kept, pltpu.SMEM((2, tiles), jnp.int32)],
        [HBM] * 4,
        [tile_row.reshape(1, tiles), tile_offset.reshape(1, tiles), vectors]
        + [tile_data.reshape(tiles // 2, 2, size, size)],
        scratch=[
            pltpu.SMEM((1, tiles), jnp.int32),
            pltpu.SMEM((1, tiles), jnp.int32),
            pltpu.SemaphoreType.DMA((tiles // chunk + 3,)),
        ],
        cost=pl.CostEstimate(flops=0, bytes_accessed=6 * tile_data.size, transcendentals=0),
    )

    flops = 2 * tiles * count * size * size
    cost = pl.CostEstimate(flops=flops, bytes_accessed=2 * tile_data.size, transcendentals=0)

    def apply(parts, slots, arrived=()):
        half = shape(F32, members, blk)
        keep_up, send_up, low = call(
            functools.partial(mirror_kernel, slots, evens),
            "mirror",
            [half, half, shape(F32, span)],
            [SMEM] * 2 + [VMEM] * (1 + len(parts)),
            [tile_live, index, tile_data, *parts],
            scratch=[
                pltpu.VMEM((span, count, size), BF16),
                pltpu.VMEM((2 * span + 1, count, size), F32),
                pltpu.VMEM((2 * span + 1, count, size), F32),
            ],
            cost=cost,
        )
        got_up = row_swap(send_up, 1)
        keep_low, send_low = call(
            functools.partial(direct_kernel, slots, evens),
            "direct",
            [half, half],
            [SMEM] * 2 + [VMEM] * (2 + len(parts) + len(arrived)),
            [tile_live, index, flipped, low, *parts, *arrived],
            scratch=[
                pltpu.VMEM((2 * span, count, size), BF16),
                pltpu.VMEM((span + 1, count, size), F32),
                pltpu.VMEM((span + 1, count, size), F32),
            ],
            cost=cost,
        )
        return (keep_up, got_up), (keep_low, row_swap(send_low, 1))

    (own,) = call(
        stack_kernel, "stack", [shape(BF16, rows, blk)], [VMEM] * rows, [vectors, *sent]
    )
    arrived = [pair_swap(own, 0), pair_swap(own, 1)]
    up, low = apply([own], [list(range(rows))], arrived)

    def coded_shape(blocks):
        return pltpu.VMEM((blocks * count + ROWS, size), jnp.int16)

    code = coded_shape(members * blk)

    def pair_sum(ours):
        paired, coded = call(
            add_kernel, "add", [shape(F32, members, blk), code], [VMEM] * 2, ours
        )
        return [paired] + [row_swap(coded, g) for g in evens[1:]]

    up = pair_sum(up)
    low = pair_sum(low)
    even, odd, total = call(
        functools.partial(gather_kernel, evens),
        "gather",
        [code] * 2 + [shape(F32, 2, members, blk)],
        [VMEM] * (2 * members),
        low + up,
    )
    (first,) = call(
        functools.partial(first_kernel, evens),
        "first",
        [shape(BF16, 2, members, blk)],
        [SMEM] * 2 + [VMEM] * 6,
        [damp_center, damp_radius, own, *arrived, total, pair_swap(odd, 1), pair_swap(even, 0)],
    )
    up, low = apply([first, row_swap(first, 1)], [evens, [s ^ 1 for s in evens]])

    spread = [shape(F32, blk)] + [coded_shape(blk)] * (members - 1)

    def pieces(ours):
        parts = call(spread_kernel, "spread", spread, [VMEM] * 2, ours)
        return parts[:1] + [row_swap(p, g) for p, g in zip(parts[1:], evens[1:])]

    up = pieces(up)
    low = pieces(low)
    (up,) = call(owner_kernel, "owner", [coded_shape(blk)], [VMEM] * members, up)
    second, first = call(
        second_kernel,
        "second",
        [jax.ShapeDtypeStruct((count, width), F32), jax.ShapeDtypeStruct((count, width), BF16)],
        [SMEM] * 2 + [VMEM] * (4 + members),
        [damp_center, damp_radius, own, first, pair_swap(up, 0), pair_swap(up, 1), *low],
    )
    return first, second


def solution(mesh):
    placed = (
        P(None, ("col", "row")),
        P(("col", "row"), None, None),
        P(("col", "row")),
        P(("col", "row")),
        P(("col", "row")),
        P(),
        P(),
    )
    return jax.shard_map(
        local,
        mesh=mesh,
        in_specs=placed,
        out_specs=(P(None, ("col", "row")), P(None, ("col", "row"))),
        check_vma=False,
    )
```

```python
import functools

import jax
import jax.numpy as jnp
from jax import lax
from jax.experimental import pallas as pl
from jax.experimental.pallas import tpu as pltpu
from jax.sharding import PartitionSpec as P

VMEM = pl.BlockSpec(memory_space=pltpu.VMEM)
SMEM = pl.BlockSpec(memory_space=pltpu.SMEM)
HBM = pl.BlockSpec(memory_space=pltpu.HBM)
AXES = ("row", "col")
F32, BF16 = jnp.float32, jnp.bfloat16


def call(kernel, name, outs, places, args, scratch=(), cost=None):
    spaces = {id(VMEM): pltpu.VMEM, id(HBM): pltpu.HBM}
    args = [
        pltpu.with_memory_space_constraint(a, spaces[id(p)]) if id(p) in spaces else a
        for a, p in zip(args, places)
    ]
    results = pl.pallas_call(
        kernel,
        out_shape=list(outs),
        in_specs=list(places),
        out_specs=[SMEM if getattr(o, "memory_space", None) == pltpu.SMEM else VMEM for o in outs],
        scratch_shapes=list(scratch),
        compiler_params=pltpu.CompilerParams(vmem_limit_bytes=12 * 1024 * 1024),
        cost_estimate=cost,
        name=name,
    )(*args)
    return list(results)


def row_swap(block, distance):
    rows, cols = lax.axis_size("row"), lax.axis_size("col")
    route = [(r * cols + c, (r ^ distance) * cols + c) for r in range(rows) for c in range(cols)]
    return lax.ppermute(block, AXES, route)


def pair_swap(block, odd):
    rows, cols = lax.axis_size("row"), lax.axis_size("col")
    route = []
    for r in range(rows):
        for c in range(cols):
            other = c + 1 if c % 2 == odd else c - 1
            other = other if 0 <= other < cols else c
            route.append((r * cols + c, (r ^ 1) * cols + other))
    return lax.ppermute(block, AXES, route)


def shift_up(block):
    rows, cols = lax.axis_size("row"), lax.axis_size("col")
    route = [(r * cols + c, (r ^ 1) * cols + (c + 1) % cols) for r in range(rows) for c in range(cols)]
    return lax.ppermute(block, AXES, route)


def by_parity(even_case, odd_case):
    parity = lax.rem(lax.axis_index("col"), 2)
    pl.when(parity == 0)(even_case)
    pl.when(parity == 1)(odd_case)


ROWS = 16


def encode(blocks, out_ref):
    parts = [block[r : r + ROWS] for block in blocks for r in range(0, block.shape[0], ROWS)]
    most = jnp.abs(parts[0])
    for part in parts[1:]:
        most = jnp.maximum(most, jnp.abs(part))
    exponent = jnp.ceil(jnp.log2(jnp.maximum(most, 1e-30)))
    scale = jnp.exp2(-exponent) * 32767.0
    for n, part in enumerate(parts):
        code = jnp.clip(jnp.round(part * scale), -32767.0, 32767.0)
        out_ref[n * ROWS : (n + 1) * ROWS] = code.astype(jnp.int32).astype(jnp.int16)
    out_ref[len(parts) * ROWS :] = exponent.astype(jnp.int32).astype(jnp.int16)


def step_of(code_ref, height):
    exponent = code_ref[code_ref.shape[0] - ROWS :].astype(jnp.int32).astype(F32)
    return jnp.concatenate([jnp.exp2(exponent) * (1.0 / 32767.0)] * (height // ROWS), axis=0)


def decode(code_ref, n, step):
    height = step.shape[0]
    return code_ref[n * height : (n + 1) * height].astype(jnp.int32).astype(F32) * step


def load_kernel(chunk, span, blk, row_hbm, offset_hbm, vectors_hbm, tile_hbm, *refs):
    kept_ref, out_ref, flipped_ref, index_ref, row_ref, offset_ref, sems = refs
    count = tile_hbm.shape[0] // chunk
    size = tile_hbm.shape[-1]
    small = [
        pltpu.make_async_copy(source, target, sems.at[2 * count + n])
        for n, (source, target) in enumerate(
            [
                (row_hbm, row_ref),
                (offset_hbm, offset_ref),
                (vectors_hbm, kept_ref),
            ]
        )
    ]

    def copies(g):
        part = pl.ds(g * chunk, chunk)
        return [
            pltpu.make_async_copy(
                tile_hbm.at[part, side],
                out_ref.at[part, :, side * size : (side + 1) * size],
                sems.at[2 * g + side],
            )
            for side in range(2)
        ]

    for one in small:
        one.start()
    for g in range(count):
        for one in copies(g):
            one.start()
    for one in small:
        one.wait()
    me = lax.axis_index("row")
    for k in range(row_ref.shape[1]):
        i = row_ref[0, k]
        j = i + offset_ref[0, k]
        index_ref[0, k] = i ^ (me * blk)
        index_ref[1, k] = jnp.where(j < span, j ^ (me * blk), span + ((j - span) ^ ((me ^ 1) * blk)))
    for g in range(count):
        for one in copies(g):
            one.wait()
        for p in range(g * chunk, (g + 1) * chunk):
            for side in range(2):
                place = slice(side * size, (side + 1) * size)
                flipped_ref[p, :, place] = out_ref[p, :, place].T


def stack_kernel(*refs):
    parts, out_ref = refs[:-1], refs[-1]
    size = out_ref.shape[-1]
    for s, part in enumerate(parts):
        for b in range(out_ref.shape[1]):
            out_ref[s, b] = part[:, b * size : (b + 1) * size]


def fill(window, half, parts, slots):
    for part, wanted in zip(parts, slots):
        for n, s in enumerate(wanted):
            blk = part.shape[-3]
            for b in range(blk):
                value = part[half, n, b] if len(part.shape) == 5 else part[n, b]
                window[s * blk + b] = value


def split(total, other, first, evens, keep_ref, send_ref):
    blk = keep_ref.shape[1]
    for n, s in enumerate(evens):
        for b in range(blk):
            kept, sent = first + s * blk + b, first + (s ^ 1) * blk + b
            keep_ref[n, b] = total[kept] + other[kept]
            send_ref[n, b] = total[sent] + other[sent]


def products(pairs_ref, window, index_ref, source, target, live_ref, *totals):
    spare = totals[0].shape[0] - 1
    for p in range(pairs_ref.shape[0]):
        stacked = jnp.concatenate([window[index_ref[source, 2 * p + side]] for side in range(2)], axis=0)
        result = jnp.dot(stacked, pairs_ref[p], preferred_element_type=F32)
        count, size = result.shape[0] // 2, result.shape[1] // 2
        for side in range(2):
            k = 2 * p + side
            to = jnp.where(k < live_ref[0], index_ref[target, k], spare)
            totals[side][to] += result[side * count : (side + 1) * count, side * size : (side + 1) * size]


def mirror_kernel(slots, evens, live_ref, index_ref, tile_ref, *refs):
    parts = refs[: len(slots)]
    keep_ref, send_ref, low_ref, window, total, other = refs[len(slots) :]
    span = window.shape[0]
    fill(window, 0, parts, slots)
    total[...] = jnp.zeros_like(total)
    other[...] = jnp.zeros_like(other)
    products(tile_ref, window, index_ref, 0, 1, live_ref, total, other)
    split(total, other, span, evens, keep_ref, send_ref)
    low_ref[...] = total[0:span] + other[0:span]


def direct_kernel(slots, evens, live_ref, index_ref, flipped_ref, low_ref, *refs):
    parts = refs[:-5]
    keep_ref, send_ref, window, total, other = refs[-5:]
    span = low_ref.shape[0]
    fill(window, 0, parts[: len(slots)], slots)
    beyond = window.at[span : 2 * span]
    if len(parts) == len(slots):
        fill(beyond, 1, parts, slots)
    else:
        even_ref, odd_ref = parts[len(slots) :]
        inside = lax.axis_index("col") < lax.axis_size("col") - 1

        def odd_case():
            fill(beyond, 1, [odd_ref], slots)

            @pl.when(jnp.logical_not(inside))
            def _():
                beyond[...] = jnp.zeros_like(beyond)

        by_parity(lambda: fill(beyond, 1, [even_ref], slots), odd_case)
    total[0:span] = low_ref[...]
    total[span] = jnp.zeros(total.shape[1:], F32)
    other[...] = jnp.zeros_like(other)
    products(flipped_ref, window, index_ref, 1, 0, live_ref, total, other)
    split(total, other, 0, evens, keep_ref, send_ref)


def add_kernel(keep_ref, got_ref, out_ref, code_ref):
    members, blk = out_ref.shape[:2]
    out_ref[...] = keep_ref[...] + got_ref[...]
    encode([out_ref[n, b] for n in range(members) for b in range(blk)], code_ref)


def gather_kernel(evens, *refs):
    members = len(evens)
    halves = refs[:members], refs[members : 2 * members]
    even_ref, odd_ref, sum_ref = refs[2 * members :]
    blk = sum_ref.shape[2]
    place = {s: n for n, s in enumerate(evens)}
    for half, (own_ref, *others) in enumerate(halves):
        steps = [step_of(other, own_ref.shape[2]) for other in others]
        for n, s in enumerate(evens):
            for b in range(blk):
                value = own_ref[n, b]
                for other, step, g in zip(others, steps, evens[1:]):
                    value = value + decode(other, place[s ^ g] * blk + b, step)
                sum_ref[half, n, b] = value

    def code(half, out_ref):
        encode([sum_ref[half, n, b] for n in range(members) for b in range(blk)], out_ref)

    def even_case():
        code(1, even_ref)
        code(0, odd_ref)

    def odd_case():
        code(0, even_ref)
        code(1, odd_ref)

    by_parity(even_case, odd_case)


def first_kernel(evens, center_ref, radius_ref, own_ref, own_even_ref, own_odd_ref, sum_ref, odd_ref, even_ref, out_ref):
    col = lax.axis_index("col")
    center, radius = center_ref[0], radius_ref[0]

    def degree(image, vectors):
        return ((image - center * vectors.astype(F32)) / radius).astype(BF16)

    def both(from_previous, from_next, next_ref):
        inside = col < lax.axis_size("col") - 1
        blk = out_ref.shape[2]
        height = out_ref.shape[3]
        previous_step, next_step = step_of(from_previous, height), step_of(from_next, height)
        for n, s in enumerate(evens):
            for b in range(blk):
                arrived = decode(from_previous, n * blk + b, previous_step)
                arrived = jnp.where(col > 0, arrived, 0.0)
                out_ref[0, n, b] = degree(sum_ref[0, n, b] + arrived, own_ref[s, b])
                arrived = decode(from_next, n * blk + b, next_step)
                beyond = degree(sum_ref[1, n, b] + arrived, next_ref[s, b])
                out_ref[1, n, b] = jnp.where(inside, beyond, jnp.zeros_like(beyond))

    by_parity(
        lambda: both(odd_ref, even_ref, own_even_ref), lambda: both(even_ref, odd_ref, own_odd_ref)
    )


def spread_kernel(keep_ref, got_ref, own_ref, *outs):
    own_ref[...] = keep_ref[0] + got_ref[0]
    for n, out_ref in enumerate(outs, 1):
        encode([keep_ref[n, b] + got_ref[n, b] for b in range(keep_ref.shape[1])], out_ref)


def total_of(own_ref, others, b):
    value = own_ref[b]
    for other in others:
        value = value + decode(other, b, step_of(other, own_ref.shape[1]))
    return value


def owner_kernel(own_ref, *refs):
    encode([total_of(own_ref, refs[:-1], b) for b in range(own_ref.shape[0])], refs[-1])


def second_kernel(center_ref, radius_ref, own_ref, first_ref, arrived_ref, low_ref, *refs):
    others, (out_ref, first_out_ref) = refs[:-2], refs[-2:]
    col = lax.axis_index("col")
    center, radius = center_ref[0], radius_ref[0]
    blk, height, size = low_ref.shape
    step = step_of(arrived_ref, height)
    for b in range(blk):
        arrived = jnp.where(col > 0, decode(arrived_ref, b, step), 0.0)
        image = total_of(low_ref, others, b) + arrived
        first = first_ref[0, 0, b]
        second = 2.0 * (image - center * first.astype(F32)) / radius - own_ref[0, b].astype(F32)
        out_ref[:, b * size : (b + 1) * size] = second
        first_out_ref[:, b * size : (b + 1) * size] = first


def local(vectors, tile_data, tile_row, tile_offset, tile_live, damp_center, damp_radius):
    rows = lax.axis_size("row")
    count, width = vectors.shape
    tiles, size, _ = tile_data.shape
    blk = width // size
    span = rows * blk
    evens = [s for s in range(rows) if bin(s).count("1") % 2 == 0]
    members = len(evens)

    def shape(dtype, *lead):
        return pltpu.VMEM((*lead, count, size), dtype)

    sent = [row_swap(vectors, s) for s in range(1, rows)]
    kept = pltpu.VMEM((tiles // 2, size, 2 * size), BF16)
    chunk = 4
    vectors, tile_data, flipped, index = call(
        functools.partial(load_kernel, chunk, span, blk),
        "load",
        [pltpu.VMEM(vectors.shape, BF16), kept, kept, pltpu.SMEM((2, tiles), jnp.int32)],
        [HBM] * 4,
        [tile_row.reshape(1, tiles), tile_offset.reshape(1, tiles), vectors]
        + [tile_data.reshape(tiles // 2, 2, size, size)],
        scratch=[
            pltpu.SMEM((1, tiles), jnp.int32),
            pltpu.SMEM((1, tiles), jnp.int32),
            pltpu.SemaphoreType.DMA((tiles // chunk + 3,)),
        ],
        cost=pl.CostEstimate(flops=0, bytes_accessed=6 * tile_data.size, transcendentals=0),
    )

    flops = 2 * tiles * count * size * size
    cost = pl.CostEstimate(flops=flops, bytes_accessed=2 * tile_data.size, transcendentals=0)

    def apply(parts, slots, arrived=()):
        half = shape(F32, members, blk)
        keep_up, send_up, low = call(
            functools.partial(mirror_kernel, slots, evens),
            "mirror",
            [half, half, shape(F32, span)],
            [SMEM] * 2 + [VMEM] * (1 + len(parts)),
            [tile_live, index, tile_data, *parts],
            scratch=[
                pltpu.VMEM((span, count, size), BF16),
                pltpu.VMEM((2 * span + 1, count, size), F32),
                pltpu.VMEM((2 * span + 1, count, size), F32),
            ],
            cost=cost,
        )
        got_up = row_swap(send_up, 1)
        keep_low, send_low = call(
            functools.partial(direct_kernel, slots, evens),
            "direct",
            [half, half],
            [SMEM] * 2 + [VMEM] * (2 + len(parts) + len(arrived)),
            [tile_live, index, flipped, low, *parts, *arrived],
            scratch=[
                pltpu.VMEM((2 * span, count, size), BF16),
                pltpu.VMEM((span + 1, count, size), F32),
                pltpu.VMEM((span + 1, count, size), F32),
            ],
            cost=cost,
        )
        return (keep_up, got_up), (keep_low, row_swap(send_low, 1))

    (own,) = call(
        stack_kernel, "stack", [shape(BF16, rows, blk)], [VMEM] * rows, [vectors, *sent]
    )
    arrived = [pair_swap(own, 0), pair_swap(own, 1)]
    up, low = apply([own], [list(range(rows))], arrived)

    def coded_shape(blocks):
        return pltpu.VMEM((blocks * count + ROWS, size), jnp.int16)

    code = coded_shape(members * blk)

    def pair_sum(ours):
        paired, coded = call(
            add_kernel, "add", [shape(F32, members, blk), code], [VMEM] * 2, ours
        )
        return [paired] + [row_swap(coded, g) for g in evens[1:]]

    up = pair_sum(up)
    low = pair_sum(low)
    even, odd, total = call(
        functools.partial(gather_kernel, evens),
        "gather",
        [code] * 2 + [shape(F32, 2, members, blk)],
        [VMEM] * (2 * members),
        low + up,
    )
    (first,) = call(
        functools.partial(first_kernel, evens),
        "first",
        [shape(BF16, 2, members, blk)],
        [SMEM] * 2 + [VMEM] * 6,
        [damp_center, damp_radius, own, *arrived, total, pair_swap(odd, 1), pair_swap(even, 0)],
    )
    up, low = apply([first, row_swap(first, 1)], [evens, [s ^ 1 for s in evens]])

    spread = [shape(F32, blk)] + [coded_shape(blk)] * (members - 1)

    def pieces(ours):
        parts = call(spread_kernel, "spread", spread, [VMEM] * 2, ours)
        return parts[:1] + [row_swap(p, g) for p, g in zip(parts[1:], evens[1:])]

    up = pieces(up)
    low = pieces(low)
    (up,) = call(owner_kernel, "owner", [coded_shape(blk)], [VMEM] * members, up)
    second, first = call(
        second_kernel,
        "second",
        [jax.ShapeDtypeStruct((count, width), F32), jax.ShapeDtypeStruct((count, width), BF16)],
        [SMEM] * 2 + [VMEM] * (3 + members),
        [damp_center, damp_radius, own, first, shift_up(up), *low],
    )
    return first, second


def solution(mesh):
    placed = (
        P(None, ("col", "row")),
        P(("col", "row"), None, None),
        P(("col", "row")),
        P(("col", "row")),
        P(("col", "row")),
        P(),
        P(),
    )
    return jax.shard_map(
        local,
        mesh=mesh,
        in_specs=placed,
        out_specs=(P(None, ("col", "row")), P(None, ("col", "row"))),
        check_vma=False,
    )
```

```python
import functools

import jax
import jax.numpy as jnp
from jax import lax
from jax.experimental import pallas as pl
from jax.experimental.pallas import tpu as pltpu
from jax.sharding import PartitionSpec as P

VMEM = pl.BlockSpec(memory_space=pltpu.VMEM)
SMEM = pl.BlockSpec(memory_space=pltpu.SMEM)
HBM = pl.BlockSpec(memory_space=pltpu.HBM)
AXES = ("row", "col")
F32, BF16 = jnp.float32, jnp.bfloat16


def call(kernel, name, outs, places, args, scratch=(), cost=None):
    spaces = {id(VMEM): pltpu.VMEM, id(HBM): pltpu.HBM}
    args = [
        pltpu.with_memory_space_constraint(a, spaces[id(p)]) if id(p) in spaces else a
        for a, p in zip(args, places)
    ]
    results = pl.pallas_call(
        kernel,
        out_shape=list(outs),
        in_specs=list(places),
        out_specs=[SMEM if getattr(o, "memory_space", None) == pltpu.SMEM else VMEM for o in outs],
        scratch_shapes=list(scratch),
        compiler_params=pltpu.CompilerParams(vmem_limit_bytes=12 * 1024 * 1024),
        cost_estimate=cost,
        name=name,
    )(*args)
    return list(results)


def row_swap(block, distance):
    rows, cols = lax.axis_size("row"), lax.axis_size("col")
    route = [(r * cols + c, (r ^ distance) * cols + c) for r in range(rows) for c in range(cols)]
    return lax.ppermute(block, AXES, route)


def pair_swap(block, odd):
    rows, cols = lax.axis_size("row"), lax.axis_size("col")
    route = []
    for r in range(rows):
        for c in range(cols):
            other = c + 1 if c % 2 == odd else c - 1
            other = other if 0 <= other < cols else c
            route.append((r * cols + c, (r ^ 1) * cols + other))
    return lax.ppermute(block, AXES, route)


def shift_up(block):
    rows, cols = lax.axis_size("row"), lax.axis_size("col")
    route = [(r * cols + c, (r ^ 1) * cols + (c + 1) % cols) for r in range(rows) for c in range(cols)]
    return lax.ppermute(block, AXES, route)


def by_parity(even_case, odd_case):
    parity = lax.rem(lax.axis_index("col"), 2)
    pl.when(parity == 0)(even_case)
    pl.when(parity == 1)(odd_case)


ROWS = 16


def encode(blocks, out_ref):
    parts = [block[r : r + ROWS] for block in blocks for r in range(0, block.shape[0], ROWS)]
    most = jnp.abs(parts[0])
    for part in parts[1:]:
        most = jnp.maximum(most, jnp.abs(part))
    exponent = jnp.ceil(jnp.log2(jnp.maximum(most, 1e-30)))
    scale = jnp.exp2(-exponent) * 32767.0
    for n, part in enumerate(parts):
        code = jnp.clip(jnp.round(part * scale), -32767.0, 32767.0)
        out_ref[n * ROWS : (n + 1) * ROWS] = code.astype(jnp.int32).astype(jnp.int16)
    out_ref[len(parts) * ROWS :] = exponent.astype(jnp.int32).astype(jnp.int16)


def step_of(code_ref, height):
    exponent = code_ref[code_ref.shape[0] - ROWS :].astype(jnp.int32).astype(F32)
    return jnp.concatenate([jnp.exp2(exponent) * (1.0 / 32767.0)] * (height // ROWS), axis=0)


def decode(code_ref, n, step):
    height = step.shape[0]
    return code_ref[n * height : (n + 1) * height].astype(jnp.int32).astype(F32) * step


def load_kernel(chunk, span, blk, row_hbm, offset_hbm, vectors_hbm, tile_hbm, *refs):
    kept_ref, out_ref, flipped_ref, index_ref, row_ref, offset_ref, sems = refs
    count = tile_hbm.shape[0] // chunk
    size = tile_hbm.shape[-1]
    small = [
        pltpu.make_async_copy(source, target, sems.at[2 * count + n])
        for n, (source, target) in enumerate(
            [
                (row_hbm, row_ref),
                (offset_hbm, offset_ref),
                (vectors_hbm, kept_ref),
            ]
        )
    ]

    def copies(g):
        part = pl.ds(g * chunk, chunk)
        return [
            pltpu.make_async_copy(
                tile_hbm.at[part, side],
                out_ref.at[part, :, side * size : (side + 1) * size],
                sems.at[2 * g + side],
            )
            for side in range(2)
        ]

    for one in small:
        one.start()
    for g in range(count):
        for one in copies(g):
            one.start()
    for one in small:
        one.wait()
    me = lax.axis_index("row")
    for k in range(row_ref.shape[1]):
        i = row_ref[0, k]
        j = i + offset_ref[0, k]
        index_ref[0, k] = i ^ (me * blk)
        index_ref[1, k] = jnp.where(j < span, j ^ (me * blk), span + ((j - span) ^ ((me ^ 1) * blk)))
    for g in range(count):
        for one in copies(g):
            one.wait()
        for p in range(g * chunk, (g + 1) * chunk):
            for side in range(2):
                place = slice(side * size, (side + 1) * size)
                flipped_ref[p, :, place] = out_ref[p, :, place].T


def stack_kernel(*refs):
    parts, out_ref = refs[:-1], refs[-1]
    size = out_ref.shape[-1]
    for s, part in zip((0, *range(len(parts) - 1, 0, -1)), parts):
        for b in range(out_ref.shape[1]):
            out_ref[s, b] = part[:, b * size : (b + 1) * size]


def fill(window, half, parts, slots):
    for part, wanted in zip(parts, slots):
        for n, s in enumerate(wanted):
            blk = part.shape[-3]
            for b in range(blk):
                value = part[half, n, b] if len(part.shape) == 5 else part[n, b]
                window[s * blk + b] = value


def split(total, other, first, evens, keep_ref, send_ref):
    blk = keep_ref.shape[1]
    for n, s in enumerate(evens):
        for b in range(blk):
            kept, sent = first + s * blk + b, first + (s ^ 1) * blk + b
            keep_ref[n, b] = total[kept] + other[kept]
            send_ref[n, b] = total[sent] + other[sent]


def products(pairs_ref, window, index_ref, source, target, live_ref, *totals):
    spare = totals[0].shape[0] - 1
    for p in range(pairs_ref.shape[0]):
        stacked = jnp.concatenate([window[index_ref[source, 2 * p + side]] for side in range(2)], axis=0)
        result = jnp.dot(stacked, pairs_ref[p], preferred_element_type=F32)
        count, size = result.shape[0] // 2, result.shape[1] // 2
        for side in range(2):
            k = 2 * p + side
            to = jnp.where(k < live_ref[0], index_ref[target, k], spare)
            totals[side][to] += result[side * count : (side + 1) * count, side * size : (side + 1) * size]


def mirror_kernel(slots, evens, live_ref, index_ref, tile_ref, *refs):
    parts = refs[: len(slots)]
    keep_ref, send_ref, low_ref, window, total, other = refs[len(slots) :]
    span = window.shape[0]
    fill(window, 0, parts, slots)
    total[...] = jnp.zeros_like(total)
    other[...] = jnp.zeros_like(other)
    products(tile_ref, window, index_ref, 0, 1, live_ref, total, other)
    split(total, other, span, evens, keep_ref, send_ref)
    low_ref[...] = total[0:span] + other[0:span]


def direct_kernel(slots, evens, live_ref, index_ref, flipped_ref, low_ref, *refs):
    parts = refs[:-5]
    keep_ref, send_ref, window, total, other = refs[-5:]
    span = low_ref.shape[0]
    fill(window, 0, parts[: len(slots)], slots)
    beyond = window.at[span : 2 * span]
    if len(parts) == len(slots):
        fill(beyond, 1, parts, slots)
    else:
        even_ref, odd_ref = parts[len(slots) :]
        inside = lax.axis_index("col") < lax.axis_size("col") - 1

        def odd_case():
            fill(beyond, 1, [odd_ref], slots)

            @pl.when(jnp.logical_not(inside))
            def _():
                beyond[...] = jnp.zeros_like(beyond)

        by_parity(lambda: fill(beyond, 1, [even_ref], slots), odd_case)
    total[0:span] = low_ref[...]
    total[span] = jnp.zeros(total.shape[1:], F32)
    other[...] = jnp.zeros_like(other)
    products(flipped_ref, window, index_ref, 1, 0, live_ref, total, other)
    split(total, other, 0, evens, keep_ref, send_ref)


def add_kernel(keep_ref, got_ref, out_ref, code_ref):
    members, blk = out_ref.shape[:2]
    out_ref[...] = keep_ref[...] + got_ref[...]
    encode([out_ref[n, b] for n in range(members) for b in range(blk)], code_ref)


def gather_kernel(evens, *refs):
    members = len(evens)
    halves = refs[:members], refs[members : 2 * members]
    even_ref, odd_ref, sum_ref = refs[2 * members :]
    blk = sum_ref.shape[2]
    place = {s: n for n, s in enumerate(evens)}
    for half, (own_ref, *others) in enumerate(halves):
        steps = [step_of(other, own_ref.shape[2]) for other in others]
        for n, s in enumerate(evens):
            for b in range(blk):
                value = own_ref[n, b]
                for other, step, g in zip(others, steps, evens[1:]):
                    value = value + decode(other, place[s ^ g] * blk + b, step)
                sum_ref[half, n, b] = value

    def code(half, out_ref):
        encode([sum_ref[half, n, b] for n in range(members) for b in range(blk)], out_ref)

    def even_case():
        code(1, even_ref)
        code(0, odd_ref)

    def odd_case():
        code(0, even_ref)
        code(1, odd_ref)

    by_parity(even_case, odd_case)


def first_kernel(evens, center_ref, radius_ref, own_ref, own_even_ref, own_odd_ref, sum_ref, odd_ref, even_ref, out_ref):
    col = lax.axis_index("col")
    center, radius = center_ref[0], radius_ref[0]

    def degree(image, vectors):
        return ((image - center * vectors.astype(F32)) / radius).astype(BF16)

    def both(from_previous, from_next, next_ref):
        inside = col < lax.axis_size("col") - 1
        blk = out_ref.shape[2]
        height = out_ref.shape[3]
        previous_step, next_step = step_of(from_previous, height), step_of(from_next, height)
        for n, s in enumerate(evens):
            for b in range(blk):
                arrived = decode(from_previous, n * blk + b, previous_step)
                arrived = jnp.where(col > 0, arrived, 0.0)
                out_ref[0, n, b] = degree(sum_ref[0, n, b] + arrived, own_ref[s, b])
                arrived = decode(from_next, n * blk + b, next_step)
                beyond = degree(sum_ref[1, n, b] + arrived, next_ref[s, b])
                out_ref[1, n, b] = jnp.where(inside, beyond, jnp.zeros_like(beyond))

    by_parity(
        lambda: both(odd_ref, even_ref, own_even_ref), lambda: both(even_ref, odd_ref, own_odd_ref)
    )


def spread_kernel(keep_ref, got_ref, own_ref, *outs):
    own_ref[...] = keep_ref[0] + got_ref[0]
    for n, out_ref in enumerate(outs, 1):
        encode([keep_ref[n, b] + got_ref[n, b] for b in range(keep_ref.shape[1])], out_ref)


def total_of(own_ref, others, b):
    value = own_ref[b]
    for other in others:
        value = value + decode(other, b, step_of(other, own_ref.shape[1]))
    return value


def owner_kernel(own_ref, *refs):
    encode([total_of(own_ref, refs[:-1], b) for b in range(own_ref.shape[0])], refs[-1])


def second_kernel(center_ref, radius_ref, own_ref, first_ref, arrived_ref, low_ref, *refs):
    others, (out_ref, first_out_ref) = refs[:-2], refs[-2:]
    col = lax.axis_index("col")
    center, radius = center_ref[0], radius_ref[0]
    blk, height, size = low_ref.shape
    step = step_of(arrived_ref, height)
    for b in range(blk):
        arrived = jnp.where(col > 0, decode(arrived_ref, b, step), 0.0)
        image = total_of(low_ref, others, b) + arrived
        first = first_ref[0, 0, b]
        second = 2.0 * (image - center * first.astype(F32)) / radius - own_ref[0, b].astype(F32)
        out_ref[:, b * size : (b + 1) * size] = second
        first_out_ref[:, b * size : (b + 1) * size] = first


def local(vectors, tile_data, tile_row, tile_offset, tile_live, damp_center, damp_radius):
    rows = lax.axis_size("row")
    count, width = vectors.shape
    tiles, size, _ = tile_data.shape
    blk = width // size
    span = rows * blk
    evens = [s for s in range(rows) if bin(s).count("1") % 2 == 0]
    members = len(evens)

    def shape(dtype, *lead):
        return pltpu.VMEM((*lead, count, size), dtype)

    sent = [row_swap(vectors, s) for s in range(1, rows)]
    kept = pltpu.VMEM((tiles // 2, size, 2 * size), BF16)
    chunk = 4
    vectors, tile_data, flipped, index = call(
        functools.partial(load_kernel, chunk, span, blk),
        "load",
        [pltpu.VMEM(vectors.shape, BF16), kept, kept, pltpu.SMEM((2, tiles), jnp.int32)],
        [HBM] * 4,
        [tile_row.reshape(1, tiles), tile_offset.reshape(1, tiles), vectors]
        + [tile_data.reshape(tiles // 2, 2, size, size)],
        scratch=[
            pltpu.SMEM((1, tiles), jnp.int32),
            pltpu.SMEM((1, tiles), jnp.int32),
            pltpu.SemaphoreType.DMA((tiles // chunk + 3,)),
        ],
        cost=pl.CostEstimate(flops=0, bytes_accessed=6 * tile_data.size, transcendentals=0),
    )

    flops = 2 * tiles * count * size * size
    cost = pl.CostEstimate(flops=flops, bytes_accessed=2 * tile_data.size, transcendentals=0)

    def apply(parts, slots, arrived=()):
        half = shape(F32, members, blk)
        keep_up, send_up, low = call(
            functools.partial(mirror_kernel, slots, evens),
            "mirror",
            [half, half, shape(F32, span)],
            [SMEM] * 2 + [VMEM] * (1 + len(parts)),
            [tile_live, index, tile_data, *parts],
            scratch=[
                pltpu.VMEM((span, count, size), BF16),
                pltpu.VMEM((2 * span + 1, count, size), F32),
                pltpu.VMEM((2 * span + 1, count, size), F32),
            ],
            cost=cost,
        )
        got_up = row_swap(send_up, 1)
        keep_low, send_low = call(
            functools.partial(direct_kernel, slots, evens),
            "direct",
            [half, half],
            [SMEM] * 2 + [VMEM] * (2 + len(parts) + len(arrived)),
            [tile_live, index, flipped, low, *parts, *arrived],
            scratch=[
                pltpu.VMEM((2 * span, count, size), BF16),
                pltpu.VMEM((span + 1, count, size), F32),
                pltpu.VMEM((span + 1, count, size), F32),
            ],
            cost=cost,
        )
        return (keep_up, got_up), (keep_low, row_swap(send_low, 1))

    (own,) = call(
        stack_kernel, "stack", [shape(BF16, rows, blk)], [VMEM] * rows, [vectors, *sent[::-1]]
    )
    arrived = [pair_swap(own, 0), pair_swap(own, 1)]
    up, low = apply([own], [list(range(rows))], arrived)

    def coded_shape(blocks):
        return pltpu.VMEM((blocks * count + ROWS, size), jnp.int16)

    code = coded_shape(members * blk)

    def pair_sum(ours):
        paired, coded = call(
            add_kernel, "add", [shape(F32, members, blk), code], [VMEM] * 2, ours
        )
        return [paired] + [row_swap(coded, g) for g in evens[1:]]

    up = pair_sum(up)
    low = pair_sum(low)
    even, odd, total = call(
        functools.partial(gather_kernel, evens),
        "gather",
        [code] * 2 + [shape(F32, 2, members, blk)],
        [VMEM] * (2 * members),
        low + up,
    )
    (first,) = call(
        functools.partial(first_kernel, evens),
        "first",
        [shape(BF16, 2, members, blk)],
        [SMEM] * 2 + [VMEM] * 6,
        [damp_center, damp_radius, own, *arrived, total, pair_swap(odd, 1), pair_swap(even, 0)],
    )
    up, low = apply([first, row_swap(first, 1)], [evens, [s ^ 1 for s in evens]])

    spread = [shape(F32, blk)] + [coded_shape(blk)] * (members - 1)

    def pieces(ours):
        parts = call(spread_kernel, "spread", spread, [VMEM] * 2, ours)
        return parts[:1] + [row_swap(p, g) for p, g in zip(parts[1:], evens[1:])]

    up = pieces(up)
    low = pieces(low)
    (up,) = call(owner_kernel, "owner", [coded_shape(blk)], [VMEM] * members, up)
    second, first = call(
        second_kernel,
        "second",
        [jax.ShapeDtypeStruct((count, width), F32), jax.ShapeDtypeStruct((count, width), BF16)],
        [SMEM] * 2 + [VMEM] * (3 + members),
        [damp_center, damp_radius, own, first, shift_up(up), *low],
    )
    return first, second


def solution(mesh):
    placed = (
        P(None, ("col", "row")),
        P(("col", "row"), None, None),
        P(("col", "row")),
        P(("col", "row")),
        P(("col", "row")),
        P(),
        P(),
    )
    return jax.shard_map(
        local,
        mesh=mesh,
        in_specs=placed,
        out_specs=(P(None, ("col", "row")), P(None, ("col", "row"))),
        check_vma=False,
    )
```
